128 devices in a mesh: seq: 16 (over z_hi, y, core), dp: 8 (over z_lo, x).
Axes of the slice: x: 4, y: 4, z: 4 (z_hi: 2, z_lo: 2; z = z_hi * 2 + z_lo), core: 2. Of those that a mesh axis runs over, the one named last changes fastest.
Arguments:
- queries: bfloat16 [8, 4096, 2048], P('dp', 'seq'), may hold values from -34 to 34
- key_heads: bfloat16 [8, 4096, 512], P('dp', 'seq'), may hold values from -7 to 7
- value_heads: bfloat16 [8, 4096, 512], P('dp', 'seq'), may hold values from -6 to 6
- doc_lengths: int32 [8, 32], P('dp'), may hold values from 1 to 256, 4096 in all within a row
- out_weight: bfloat16 [2048, 2048], P('dp'), may hold values from -0.125 to 0.125
- cotangent: bfloat16 [8, 4096, 2048], P('dp', 'seq'), may hold values from -6 to 6
Outputs:
- projected: bfloat16 [8, 4096, 2048], P('dp', 'seq')
- grad_queries: bfloat16 [8, 4096, 2048], P('dp', 'seq')
- grad_keys: bfloat16 [8, 4096, 512], P('dp', 'seq')
- grad_values: bfloat16 [8, 4096, 512], P('dp', 'seq')
- grad_weight: float32 [2048, 2048], P('dp')
The draws below stay inside these ranges and needn't reach their ends.
Inputs may be any that keep to these rules, and one draw needn't show every extreme that they name: `doc_lengths`: each pack's documents lie end to end in this order and fill its 4096 tokens; no document is longer than 256 tokens, and in every pack one document is exactly that long.
All inputs are finite; a program needn't handle non-finite values.
Results may differ from the reference program's by a relative error of at most 0.017.
Values may be sent and summed in bfloat16 or wider, within the bound.
A program may use at most 128 MiB of HBM per device.

```python
import math
import jax
import jax.numpy as jnp
import numpy as np
from jax import lax

HQ = 16
HK = 4
DH = 128
DM = 2048
TOK_DEV = 256
QW = 2048
KW = 512
SEQ = 4096
PACKS = 8
DOCS = 32
N_SEQ = 16


def paired_draw(key):
    group = HQ // HK
    key_query = jax.random.fold_in(key, 101)
    key_key = jax.random.fold_in(key, 102)
    key_rows = jnp.clip(jax.random.normal(key_key, (PACKS, SEQ, HK, DH), jnp.float32), -6.0, 6.0)
    query_rows = jnp.clip(jax.random.normal(key_query, (PACKS, SEQ, HK, group, DH), jnp.float32), -6.0, 6.0)
    return (query_rows.reshape(PACKS, SEQ, HK * group * DH), key_rows.reshape(PACKS, SEQ, HK * DH))


def draw_queries(key, part):
    return paired_draw(key)[0].astype(jnp.bfloat16)


def draw_key_heads(key, part):
    return paired_draw(key)[1].astype(jnp.bfloat16)


def shard_levels(key, shape, pieces, smallest, largest):
    factor_of = 1.0
    for axis_at, blocks in pieces:
        steps = jax.random.uniform(jax.random.fold_in(jax.random.fold_in(key, 6), axis_at), (blocks,), jnp.float32, smallest / len(pieces), largest / len(pieces))
        factor_of = factor_of * jnp.repeat(jnp.exp(steps), shape[axis_at] // blocks).reshape((-1,) + (1,) * (len(shape) - 1 - axis_at))
    return factor_of


def split_up(number_of, total, bound, lean):
    weights = [(1 << 20) // math.isqrt(rank ** lean) + 1 for rank in range(2, number_of + 1)]
    spare, given = total - bound - (number_of - 1), [1] * (number_of - 1)
    while spare > 0:
        movable = [i for i in range(number_of - 1) if given[i] < bound]
        whole, budget = sum([weights[i] for i in movable]), spare
        for i in movable:
            more = min(bound - given[i], max(1, budget * weights[i] // whole), spare)
            given[i] = given[i] + more
            spare = spare - more
    return np.array([bound] + given)


def ragged(stream_key, count, total, bound, slope):
    if count == 2:
        one = jax.random.randint(stream_key, (), max(1, total - bound), min(bound, total - 1) + 1)
        return jnp.stack([one, total - one])
    tallies = jnp.asarray(split_up(count, total, bound, slope), jnp.int32)
    couples = (count - 1) // 2
    giver, taker = tallies[1:1 + 2 * couples:2], tallies[2:2 + 2 * couples:2]
    margin = jnp.minimum(giver - 1, bound - taker)
    moved = jax.random.randint(jax.random.fold_in(stream_key, 1), (couples,), 0, 1 << 20) % (margin + 1)
    tallies = tallies.at[1:1 + 2 * couples:2].set(giver - moved).at[2:2 + 2 * couples:2].set(taker + moved)
    return tallies[jax.random.permutation(jax.random.fold_in(stream_key, 2), count)]


def centred(own_key, shape, width, limit, pieces=(), kind=jnp.bfloat16):
    values = width * jax.random.normal(own_key, shape, jnp.float32)
    if pieces:
        values = values * shard_levels(own_key, shape, pieces, -0.22, 0.18)
    return jnp.clip(values, -limit, limit).astype(kind)


def setup_inputs(seed: int = 0) -> dict:
    streams_of = jax.random.split(jax.random.key(seed), 7)
    queries = draw_queries(jax.random.fold_in(streams_of[6], 71), 0)
    key_heads = draw_key_heads(jax.random.fold_in(streams_of[6], 71), 0)
    value_heads = centred(streams_of[2], (PACKS, SEQ, KW), 1.0, 6.0, ((0, 8), (1, 16)))
    doc_lengths = jax.vmap(lambda own: ragged(own, DOCS, SEQ, TOK_DEV, 1))(jax.random.split(streams_of[3], PACKS)).reshape((PACKS, DOCS)).astype(jnp.int32)
    out_weight = centred(streams_of[4], (QW, DM), QW ** -0.5, 0.125, ((0, 8),))
    cotangent = centred(streams_of[5], (PACKS, SEQ, DM), 1.0, 6.0, ((0, 8), (1, 16)))
    return {"queries": queries, "key_heads": key_heads, "value_heads": value_heads, "doc_lengths": doc_lengths, "out_weight": out_weight, "cotangent": cotangent}


def doc_begin(lengths, position):
    ending = jnp.cumsum(lengths).astype(jnp.int32)
    opening = (ending - lengths).astype(jnp.int32)
    covered = opening[None, :] <= position[:, None]
    return lax.optimization_barrier(jnp.max(jnp.where(covered, opening[None, :], 0), axis=-1)).astype(jnp.int32)

def attend_block(query, key_block, value_block, grad_att, q_begin, q_pos, k_pos):
    rows = query.shape[0]
    span = key_block.shape[0]
    group = HQ // HK
    scale = 1.0 / math.sqrt(DH)
    q_heads = query.reshape(rows, HK, group, DH).astype(jnp.float32)
    k_heads = key_block.reshape(span, HK, DH).astype(jnp.float32)
    v_heads = value_block.reshape(span, HK, DH).astype(jnp.float32)
    g_heads = grad_att.reshape(rows, HK, group, DH).astype(jnp.float32)
    scores = jnp.einsum('ikgd,jkd->kgij', q_heads, k_heads) * scale
    allowed = (k_pos[None, :] >= q_begin[:, None]) & (k_pos[None, :] <= q_pos[:, None])
    scores = jnp.where(allowed, scores, -jnp.inf)
    peak = lax.optimization_barrier(jnp.max(scores, axis=-1, keepdims=True))
    logsum = peak + jnp.log(lax.optimization_barrier(jnp.sum(jnp.exp(scores - peak), axis=-1, keepdims=True)))
    probs = jnp.exp(scores - logsum)
    probs_low = lax.optimization_barrier(probs.astype(jnp.bfloat16))
    attended = jnp.einsum('kgij,jkd->ikgd', probs_low.astype(jnp.float32), v_heads).astype(jnp.bfloat16)
    delta = jnp.einsum('ikgd,ikgd->kgi', g_heads, attended.astype(jnp.float32))
    grad_probs = jnp.einsum('ikgd,jkd->kgij', g_heads, v_heads)
    grad_low = lax.optimization_barrier((probs * (grad_probs - delta[..., None])).astype(jnp.bfloat16))
    grad_scores = grad_low.astype(jnp.float32)
    grad_query = (jnp.einsum('kgij,jkd->ikgd', grad_scores, k_heads) * scale).astype(jnp.bfloat16)
    grad_key = jnp.einsum('kgij,ikgd->jkd', grad_scores, q_heads) * scale
    grad_value = jnp.einsum('kgij,ikgd->jkd', probs_low.astype(jnp.float32), g_heads)
    return (attended.reshape(rows, HK * group * DH), grad_query.reshape(rows, HK * group * DH), grad_key.reshape(span, HK * DH), grad_value.reshape(span, HK * DH))

def reference(queries, key_heads, value_heads, doc_lengths, out_weight, cotangent):
    position = jnp.arange(SEQ, dtype=jnp.int32)

    def pack_begin(lengths):
        return doc_begin(lengths, position)
    begins = jax.vmap(pack_begin)(doc_lengths)
    flat_cot = cotangent.reshape(PACKS * SEQ, DM)
    grad_att = jnp.dot(flat_cot, out_weight.T, preferred_element_type=jnp.float32).astype(jnp.bfloat16)
    grad_att = grad_att.reshape(PACKS, SEQ, QW)
    padding = jnp.zeros((PACKS, TOK_DEV, KW), jnp.bfloat16)
    key_pad = jnp.concatenate([padding, key_heads], axis=1)
    value_pad = jnp.concatenate([padding, value_heads], axis=1)

    def one_block(index):
        pack = (index // N_SEQ).astype(jnp.int32)
        block = (index % N_SEQ).astype(jnp.int32)
        offset = (block * TOK_DEV).astype(jnp.int32)

        def select(array):
            return lax.dynamic_index_in_dim(array, pack, 0, keepdims=False)
        query = lax.dynamic_slice_in_dim(select(queries), offset, TOK_DEV, 0)
        key_block = lax.dynamic_slice_in_dim(select(key_pad), offset, 2 * TOK_DEV, 0)
        value_block = lax.dynamic_slice_in_dim(select(value_pad), offset, 2 * TOK_DEV, 0)
        grad_block = lax.dynamic_slice_in_dim(select(grad_att), offset, TOK_DEV, 0)
        q_begin = lax.dynamic_slice_in_dim(select(begins), offset, TOK_DEV, 0)
        q_pos = (offset + jnp.arange(TOK_DEV, dtype=jnp.int32)).astype(jnp.int32)
        k_pos = (offset - TOK_DEV + jnp.arange(2 * TOK_DEV, dtype=jnp.int32)).astype(jnp.int32)
        return attend_block(query, key_block, value_block, grad_block, q_begin, q_pos, k_pos)
    attended, grad_q, grad_k, grad_v = lax.map(one_block, jnp.arange(PACKS * N_SEQ, dtype=jnp.int32))

    def settle(part):
        part = part.reshape(PACKS, N_SEQ, 2 * TOK_DEV, KW)
        earlier = part[:, :, :TOK_DEV]
        own_part = part[:, :, TOK_DEV:]
        carried = jnp.concatenate([earlier[:, 1:], jnp.zeros_like(earlier[:, :1])], axis=1)
        return (own_part + carried).astype(jnp.bfloat16).reshape(PACKS, SEQ, KW)
    attended = attended.reshape(PACKS * SEQ, QW)
    projected = jnp.dot(attended, out_weight, preferred_element_type=jnp.float32).astype(jnp.bfloat16)
    grad_weight = jnp.dot(attended.T, flat_cot, preferred_element_type=jnp.float32) * (1.0 / math.sqrt(PACKS * SEQ))
    return (projected.reshape(PACKS, SEQ, DM), grad_q.reshape(PACKS, SEQ, QW), settle(grad_k), settle(grad_v), grad_weight)
```

```python
import math

import jax
import jax.numpy as jnp
from jax import lax
from jax.experimental import pallas as pl
from jax.experimental.pallas import tpu as pltpu
from jax.sharding import PartitionSpec as P

HQ = 16
HK = 4
DH = 128
DM = 2048
TOK = 256
DOCS = 32
TOTAL = 32768
SCALE = 1.0 / math.sqrt(DH)
F32 = jnp.float32
BF16 = jnp.bfloat16
MESH = pl.DeviceIdType.MESH

HALO = 0
WX = HALO + 2
WZ = WX + 3
WC = WZ + 8
COT = WC + 7
ATT = COT + 1
Y1 = ATT + 4
X1 = Y1 + 12
Z1 = X1 + 3
Y2 = Z1 + 3
X2 = Y2 + 3
Z2 = X2 + 3
Y3 = Z2 + 3
X3 = Y3 + 3
Z3 = X3 + 3
BACK = Z3 + 3
AG = BACK + 2
AGC = AG + 7
COPIES = AGC + 8


def dg(a, b, ca, cb):
    return lax.dot_general(a, b, (((ca,), (cb,)), ((), ())), preferred_element_type=F32)


def kernel(
    len_ref, q_hbm, k_hbm, v_hbm, w_hbm, cot_hbm,
    pro_hbm, gq_hbm, gk_hbm, gv_hbm, gw_hbm,
    q_v, cot_v, kv, wf, cotm, att, attm, prob, bias,
    g_y, r_y1, s_y, r_y2, s_y2, r_y3,
    g_x, r_x1, s_x, r_x2, s_x2, r_x3,
    g_z, r_z1, s_z, r_z2, s_z2, r_z3,
    agb, gk_t, gv_t, back_s, back_r,
    pro_v, gq_v, gkv_v, gw_v,
    ssem, rsem, lsem, osem,
):
    s = lax.axis_index("seq")
    d = lax.axis_index("dp")
    zh = lax.div(s, 8)
    y = lax.rem(lax.div(s, 2), 4)
    c = lax.rem(s, 2)
    zl = lax.div(d, 4)
    x = lax.rem(d, 4)
    z = zh * 2 + zl

    def at(zh_, y_, c_, zl_, x_):
        return {"seq": zh_ * 8 + y_ * 2 + c_, "dp": zl_ * 4 + x_}

    def turn(v, n):
        return lax.rem(v + n, 4)

    def to_x(n):
        return at(zh, y, c, zl, turn(x, n))

    def to_y(n):
        return at(zh, turn(y, n), c, zl, x)

    def to_z(n):
        zz = turn(z, n)
        return at(lax.div(zz, 2), y, c, lax.rem(zz, 2), x)

    def to_o(n):
        return at(1 - zh, turn(y, n), c, zl, x)

    mate = at(zh, y, 1 - c, zl, x)
    near = at(zh, y, c, 1 - zl, x)
    far = at(1 - zh, y, c, 1 - zl, x)
    after = {"seq": lax.rem(s + 1, 16), "dp": d}
    before = {"seq": lax.rem(s + 15, 16), "dp": d}

    def rc(n, src, dst, to):
        return pltpu.make_async_remote_copy(
            src_ref=src, dst_ref=dst, send_sem=ssem.at[n], recv_sem=rsem.at[n],
            device_id=to, device_id_type=MESH,
        )

    sent = []

    def send(n, src, dst, to):
        copy = rc(n, src, dst, to)
        copy.start()
        sent.append(copy)

    loads = [
        pltpu.make_async_copy(k_hbm, kv.at[0, pl.ds(TOK, TOK)], lsem.at[0]),
        pltpu.make_async_copy(v_hbm, kv.at[1, pl.ds(TOK, TOK)], lsem.at[1]),
        pltpu.make_async_copy(q_hbm, q_v, lsem.at[2]),
        pltpu.make_async_copy(cot_hbm, cot_v, lsem.at[3]),
        pltpu.make_async_copy(w_hbm, wf.at[d], lsem.at[4]),
    ]
    for load in loads:
        load.start()

    barrier = pltpu.get_barrier_semaphore()
    peers = [mate, after, before]
    peers += [f(n) for f in (to_x, to_y, to_z) for n in (1, 2, 3)]
    peers += [to_o(n) for n in (1, 2, 3)]
    for peer in peers:
        pl.semaphore_signal(barrier, inc=1, device_id=peer, device_id_type=MESH)
    pl.semaphore_wait(barrier, len(peers))

    prev = pl.ds(0, TOK)
    send(HALO, k_hbm, kv.at[0, prev], after)
    send(HALO + 1, v_hbm, kv.at[1, prev], after)
    way = (1, 3, 2)
    for i, n in enumerate(way):
        send(WX + i, w_hbm.at[c], wf.at[d, c], to_x(n))
    low, high = pl.ds(0, 64), pl.ds(64, 64)
    send(WZ, w_hbm.at[c, low], wf.at[d, c, low], near)
    send(WZ + 1, w_hbm.at[c, high], wf.at[d, c, high], far)
    send(COT, cot_hbm.at[:, pl.ds(pl.multiple_of((1 - c) * 1024, 1024), 1024)], cotm, mate)

    def shard_x(i, plane):
        return plane * 4 + (x if i == 0 else turn(x, 4 - way[i - 1]))

    def forward_x(i):
        e = shard_x(i, zl)
        rc(WX + i - 1, w_hbm.at[c], wf.at[e, c], mate).wait_recv()
        send(WZ + 2 * i, wf.at[e, c, low], wf.at[e, c, low], near)
        send(WZ + 2 * i + 1, wf.at[e, c, high], wf.at[e, c, high], far)
        send(WC + i - 1, wf.at[e, c], wf.at[e, c], mate)

    def forward_z(i):
        e = shard_x(i, 1 - zl)
        rc(WZ + 2 * i, w_hbm.at[c, low], wf.at[e, c, low], mate).wait_recv()
        rc(WZ + 2 * i + 1, w_hbm.at[c, high], wf.at[e, c, high], mate).wait_recv()
        send(WC + 3 + i, wf.at[e, c], wf.at[e, c], mate)

    def from_mate(j, e):
        rc(WC + j, wf.at[e, 1 - c], wf.at[e, 1 - c], mate).wait_recv()

    first = s * TOK
    q_pos = first + lax.broadcasted_iota(jnp.int32, (TOK, 1), 0)
    begin = jnp.zeros((TOK, 1), jnp.int32)
    opening = len_ref[0, 0] * 0
    for n in range(DOCS):
        begin = jnp.where(q_pos >= opening, opening, begin)
        opening = opening + len_ref[0, n]
    k_pos = first - TOK + lax.broadcasted_iota(jnp.int32, (TOK, 2 * TOK), 1)
    bias[...] = jnp.where((k_pos >= begin) & (k_pos <= q_pos), 0.0, -1e30)
    gk_t[...] = jnp.zeros_like(gk_t)
    gv_t[...] = jnp.zeros_like(gv_t)

    for load in loads:
        load.wait()
    rc(HALO, k_hbm, kv.at[0, prev], after).wait_recv()
    rc(HALO + 1, v_hbm, kv.at[1, prev], after).wait_recv()

    def head(h):
        return pl.ds(pl.multiple_of(h * DH, DH), DH)

    def fwd(k):
        keys, values = kv[0, :, head(k)], kv[1, :, head(k)]

        def one(g, _):
            h = k * 4 + g
            scores = dg(q_v[:, head(h)], keys, 1, 1) * SCALE + bias[...]
            e = jnp.exp(scores - jnp.max(scores, axis=-1, keepdims=True))
            p = (e * (1.0 / jnp.sum(e, axis=-1, keepdims=True))).astype(BF16)
            prob[h] = p
            att[:, head(h)] = dg(p, values, 1, 0).astype(BF16)
            return 0

        lax.fori_loop(0, 4, one, 0)
        cols = pl.ds(k * 512, 512)
        send(ATT + k, att.at[:, cols], attm.at[:, cols], mate)

    def grad_w(k):
        cols = pl.ds(k * 512, 512)
        rc(ATT + k, att.at[:, cols], attm.at[:, cols], mate).wait_recv()
        if k == 0:
            rc(COT, cotm, cotm, mate).wait_recv()
        for e in (2 * k, 2 * k + 1):
            own = att[:, e * 256 : (e + 1) * 256]
            other = attm[:, e * 256 : (e + 1) * 256]
            for n in range(4):
                mine = cot_v[:, pl.ds(pl.multiple_of(c * 1024 + n * 256, 256), 256)]
                part = dg(own, mine, 0, 0) + dg(other, cotm[:, n * 256 : (n + 1) * 256], 0, 0)
                part = part.astype(BF16)
                for sub in range(8):
                    rows = part[sub * 32 : (sub + 1) * 32]
                    if n < 2:
                        g_y[sub % 4, e, sub // 4, :, n * 256 : (n + 1) * 256] = rows
                    elif n == 2:
                        g_x[e % 4, e // 4, sub] = rows
                    else:
                        g_z[sub // 4 * 2 + e // 4, e % 4, sub % 4] = rows
        both = pl.ds(2 * k, 2)
        for n in (1, 3, 2):
            send(Y1 + 3 * k + n - 1, g_y.at[turn(y, n), both], r_y1.at[n - 1, both], to_y(n))

    for k in range(HK):
        fwd(k)
        if k > 0:
            grad_w(k - 1)
        if k == 2:
            forward_x(1)
        if k == 3:
            forward_x(2)
    grad_w(HK - 1)
    forward_x(3)
    for n in (1, 3, 2):
        send(X1 + n - 1, g_x.at[turn(x, n)], r_x1.at[n - 1], to_x(n))
        send(Z1 + n - 1, g_z.at[turn(z, n)], r_z1.at[n - 1], to_z(n))

    def bwd(e):
        k = lax.div(e, 2)
        weight = wf[e].reshape(256, DM)
        grad = dg(cot_v[...], weight, 1, 1).astype(BF16)
        keys, values = kv[0, :, head(k)], kv[1, :, head(k)]
        for g in range(2):
            h = 2 * e + g
            grad_h = grad[:, g * DH : (g + 1) * DH]
            delta = jnp.sum(
                grad_h.astype(F32) * att[:, head(h)].astype(F32), axis=-1, keepdims=True
            )
            p = prob[h]
            grad_s = (p.astype(F32) * (dg(grad_h, values, 1, 1) - delta)).astype(BF16)
            gq_v[:, head(h)] = (dg(grad_s, keys, 1, 0) * SCALE).astype(BF16)
            gk_t[head(k), :] += dg(q_v[:, head(h)], grad_s, 0, 0)
            gv_t[head(k), :] += dg(grad_h, p, 0, 0)

    bwd(d)
    for i in range(1, 4):
        e = shard_x(i, zl)
        if i == 1:
            forward_z(0)
        from_mate(i - 1, e)
        bwd(e)
    for i in range(4):
        e = shard_x(i, 1 - zl)
        if i < 3:
            forward_z(i + 1)
        from_mate(3 + i, e)
        bwd(e)

    back_s[0] = (gk_t[:, 0:TOK].T * SCALE).astype(BF16)
    back_s[1] = gv_t[:, 0:TOK].T.astype(BF16)
    send(BACK, back_s.at[0], back_r.at[0], before)
    send(BACK + 1, back_s.at[1], back_r.at[1], before)

    def arrived(base, dst, source):
        for n in range(3):
            rc(base + n, source, dst.at[n], mate).wait_recv()

    def total(own, got, *where):
        out = own.astype(F32)
        for n in range(3):
            out = out + got[(n, *where)].astype(F32)
        return out

    arrived(X1, r_x1, g_x.at[0])
    for zl_ in range(2):
        for sub in range(8):
            value = total(g_x[x, zl_, sub], r_x1, zl_, sub)
            s_x[sub // 4 * 2 + zl_, sub % 4] = value.astype(BF16)
    for n in (1, 3, 2):
        send(Z2 + n - 1, s_x.at[turn(z, n)], r_x2.at[n - 1], to_z(n))

    arrived(Z1, r_z1, g_z.at[0])
    for x_ in range(4):
        for y_ in range(4):
            s_z[y_, x_] = total(g_z[z, x_, y_], r_z1, x_, y_).astype(BF16)
    for n in (1, 3, 2):
        send(Y2 + n - 1, s_z.at[turn(y, n)], r_z2.at[n - 1], to_y(n))

    for k in range(HK):
        both = pl.ds(2 * k, 2)
        for n in range(3):
            rc(Y1 + 3 * k + n, g_y.at[0, both], r_y1.at[n, both], mate).wait_recv()
    for e in range(8):
        for zh_ in range(2):
            s_y[e % 4, e // 4, zh_] = total(g_y[y, e, zh_], r_y1, e, zh_).astype(BF16)
    for n in (1, 3, 2):
        send(X2 + n - 1, s_y.at[turn(x, n)], r_y2.at[n - 1], to_x(n))

    def project(n, _):
        cols = pl.ds(pl.multiple_of(n * 256, 256), 256)
        weight = wf[:, :, :, cols].reshape(2048, 256)
        pro_v[:, cols] = dg(att[...], weight, 1, 0).astype(BF16)
        return 0

    lax.fori_loop(0, 8, project, 0)
    outs = [
        pltpu.make_async_copy(pro_v, pro_hbm, osem.at[0]),
        pltpu.make_async_copy(gq_v, gq_hbm, osem.at[1]),
    ]
    for out in outs:
        out.start()

    arrived(Z2, r_x2, s_x.at[0])
    for y_ in range(4):
        s_x2[y_] = total(s_x[z, y_], r_x2, y_).astype(BF16)
    for n in (1, 3, 2):
        send(Y3 + n - 1, s_x2.at[turn(y, n)], r_x3.at[n - 1], to_y(n))
    arrived(Y2, r_z2, s_z.at[0])
    for x_ in range(4):
        s_z2[x_] = total(s_z[y, x_], r_z2, x_).astype(BF16)
    for n in (1, 3, 2):
        send(X3 + n - 1, s_z2.at[turn(x, n)], r_z3.at[n - 1], to_x(n))
    arrived(X2, r_y2, s_y.at[0])
    for zl_ in range(2):
        for zh_ in range(2):
            s_y2[zh_ * 2 + zl_] = total(s_y[x, zl_, zh_], r_y2, zl_, zh_).astype(BF16)
    for n in (1, 3, 2):
        send(Z3 + n - 1, s_y2.at[turn(z, n)], r_y3.at[n - 1], to_z(n))

    factor = 1.0 / math.sqrt(TOTAL)
    mine = zh * 4 + y
    arrived(Y3, r_x3, s_x2.at[0])
    agb[c, mine, :, 512:768] = (total(s_x2[y], r_x3) * factor).astype(BF16)
    arrived(X3, r_z3, s_z2.at[0])
    agb[c, mine, :, 768:1024] = (total(s_z2[x], r_z3) * factor).astype(BF16)
    arrived(Z3, r_y3, s_y2.at[0])
    agb[c, mine, :, 0:512] = (total(s_y2[z], r_y3) * factor).astype(BF16)

    for n in range(7):
        to = to_y(n + 1) if n < 3 else to_o(n - 3)
        send(AG + n, agb.at[c, mine], agb.at[c, mine], to)
    send(AGC + 7, agb.at[c, mine], agb.at[c, mine], mate)

    rc(BACK, back_s.at[0], back_r.at[0], before).wait_recv()
    rc(BACK + 1, back_s.at[1], back_r.at[1], before).wait_recv()
    gkv_v[0] = (gk_t[:, TOK : 2 * TOK].T * SCALE + back_r[0].astype(F32)).astype(BF16)
    gkv_v[1] = (gv_t[:, TOK : 2 * TOK].T + back_r[1].astype(F32)).astype(BF16)
    for n, out in enumerate((gk_hbm, gv_hbm)):
        outs.append(pltpu.make_async_copy(gkv_v.at[n], out, osem.at[2 + n]))
        outs[-1].start()

    def origin(n):
        if n == 7:
            return mine
        return zh * 4 + turn(y, 3 - n) if n < 3 else (1 - zh) * 4 + turn(y, 7 - n)

    for n in range(7):
        piece = agb.at[c, origin(n)]
        rc(AG + n, piece, piece, mate).wait_recv()
        send(AGC + n, piece, piece, mate)
    for n in range(8):
        piece = agb.at[1 - c, origin(n)]
        rc(AGC + n, piece, piece, mate).wait_recv()
    for sub in range(8):
        for half in range(2):
            gw_v[sub * 32 : (sub + 1) * 32, half * 1024 : (half + 1) * 1024] = agb[
                half, sub
            ].astype(F32)
    outs.append(pltpu.make_async_copy(gw_v, gw_hbm, osem.at[4]))
    outs[-1].start()
    for copy in sent:
        copy.wait_send()
    for out in outs:
        out.wait()


def body(queries, key_heads, value_heads, doc_lengths, out_weight, cotangent):
    anywhere = pl.BlockSpec(memory_space=pl.ANY)
    shapes = [
        ((TOK, 2048), BF16),
        ((TOK, 2048), BF16),
        ((2, 512, 512), BF16),
        ((8, 2, 128, 2048), BF16),
        ((TOK, 1024), BF16),
        ((TOK, 2048), BF16),
        ((TOK, 2048), BF16),
        ((HQ, TOK, 512), BF16),
        ((TOK, 512), F32),
        ((4, 8, 2, 32, 512), BF16),
        ((3, 8, 2, 32, 512), BF16),
        ((4, 2, 2, 32, 512), BF16),
        ((3, 2, 2, 32, 512), BF16),
        ((4, 32, 512), BF16),
        ((3, 32, 512), BF16),
        ((4, 2, 8, 32, 256), BF16),
        ((3, 2, 8, 32, 256), BF16),
        ((4, 4, 32, 256), BF16),
        ((3, 4, 32, 256), BF16),
        ((4, 32, 256), BF16),
        ((3, 32, 256), BF16),
        ((4, 4, 4, 32, 256), BF16),
        ((3, 4, 4, 32, 256), BF16),
        ((4, 4, 32, 256), BF16),
        ((3, 4, 32, 256), BF16),
        ((4, 32, 256), BF16),
        ((3, 32, 256), BF16),
        ((2, 8, 32, 1024), BF16),
        ((512, 512), F32),
        ((512, 512), F32),
        ((2, TOK, 512), BF16),
        ((2, TOK, 512), BF16),
        ((TOK, 2048), BF16),
        ((TOK, 2048), BF16),
        ((2, TOK, 512), BF16),
        ((TOK, 2048), F32),
    ]
    scratch = [pltpu.VMEM(shape, dtype) for shape, dtype in shapes]
    scratch += [pltpu.SemaphoreType.DMA((n,)) for n in (COPIES, COPIES, 5, 5)]
    outs = pl.pallas_call(
        kernel,
        out_shape=[
            jax.ShapeDtypeStruct((TOK, 2048), BF16),
            jax.ShapeDtypeStruct((TOK, 2048), BF16),
            jax.ShapeDtypeStruct((TOK, 512), BF16),
            jax.ShapeDtypeStruct((TOK, 512), BF16),
            jax.ShapeDtypeStruct((TOK, 2048), F32),
        ],
        in_specs=[pl.BlockSpec(memory_space=pltpu.SMEM)] + [anywhere] * 5,
        out_specs=[anywhere] * 5,
        scratch_shapes=scratch,
        compiler_params=pltpu.CompilerParams(
            collective_id=0, has_side_effects=True, vmem_limit_bytes=56 << 20
        ),
        cost_estimate=pl.CostEstimate(
            flops=10_000_000_000, bytes_accessed=12_000_000, transcendentals=2_000_000
        ),
    )(
        doc_lengths,
        queries[0],
        key_heads[0],
        value_heads[0],
        out_weight.reshape(2, 128, DM),
        cotangent[0],
    )
    return (*(out[None] for out in outs[:4]), outs[4])


def solution(mesh):
    tokens = P("dp", "seq", None)
    rows = P("dp", None)
    return jax.shard_map(
        body,
        mesh=mesh,
        in_specs=(tokens, tokens, tokens, rows, rows, tokens),
        out_specs=(tokens, tokens, tokens, tokens, rows),
        check_vma=False,
    )
```

```python
import math

import jax
import jax.numpy as jnp
from jax import lax
from jax.experimental import pallas as pl
from jax.experimental.pallas import tpu as pltpu
from jax.sharding import PartitionSpec as P

HQ = 16
HK = 4
DH = 128
DM = 2048
TOK = 256
DOCS = 32
TOTAL = 32768
SCALE = 1.0 / math.sqrt(DH)
F32 = jnp.float32
BF16 = jnp.bfloat16
MESH = pl.DeviceIdType.MESH

HALO = 0
WX = HALO + 8
WZ = WX + 6
WC = WZ + 8
COT = WC + 7
ATT = COT + 1
Y1 = ATT + 4
X1 = Y1 + 12
Z1 = X1 + 3
Y2 = Z1 + 3
X2 = Y2 + 3
Z2 = X2 + 3
Y3 = Z2 + 3
X3 = Y3 + 3
Z3 = X3 + 3
BACK = Z3 + 3
AG = BACK + 2
AGC = AG + 14
COPIES = AGC + 2


def dg(a, b, ca, cb):
    return lax.dot_general(a, b, (((ca,), (cb,)), ((), ())), preferred_element_type=F32)


def kernel(
    len_ref, q_hbm, k_hbm, v_hbm, w_hbm, cot_hbm,
    pro_hbm, gq_hbm, gk_hbm, gv_hbm, gw_hbm,
    q_v, cot_v, kv, wf, cotm, att, attm, prob, bias,
    g_y, r_y1, s_y, r_y2, s_y2, r_y3,
    g_x, r_x1, s_x, r_x2, s_x2, r_x3,
    g_z, r_z1, s_z, r_z2, s_z2, r_z3,
    agb, gk_t, gv_t, back_s, back_r,
    pro_v, gq_v, gkv_v,
    ssem, rsem, lsem, osem,
):
    s = lax.axis_index("seq")
    d = lax.axis_index("dp")
    zh = lax.div(s, 8)
    y = lax.rem(lax.div(s, 2), 4)
    c = lax.rem(s, 2)
    zl = lax.div(d, 4)
    x = lax.rem(d, 4)
    z = zh * 2 + zl

    def at(zh_, y_, c_, zl_, x_):
        return {"seq": zh_ * 8 + y_ * 2 + c_, "dp": zl_ * 4 + x_}

    def turn(v, n):
        return lax.rem(v + n, 4)

    def to_x(n):
        return at(zh, y, c, zl, turn(x, n))

    def to_y(n):
        return at(zh, turn(y, n), c, zl, x)

    def to_z(n):
        zz = turn(z, n)
        return at(lax.div(zz, 2), y, c, lax.rem(zz, 2), x)

    def to_o(n):
        return at(1 - zh, turn(y, n), c, zl, x)

    mate = at(zh, y, 1 - c, zl, x)
    near = at(zh, y, c, 1 - zl, x)
    far = at(1 - zh, y, c, 1 - zl, x)
    after = {"seq": lax.rem(s + 1, 16), "dp": d}
    before = {"seq": lax.rem(s + 15, 16), "dp": d}

    def rc(n, src, dst, to):
        return pltpu.make_async_remote_copy(
            src_ref=src, dst_ref=dst, send_sem=ssem.at[n], recv_sem=rsem.at[n],
            device_id=to, device_id_type=MESH,
        )

    sent = []

    def send(n, src, dst, to):
        copy = rc(n, src, dst, to)
        copy.start()
        sent.append(copy)

    loads = [
        pltpu.make_async_copy(k_hbm, kv.at[0, pl.ds(TOK, TOK)], lsem.at[0]),
        pltpu.make_async_copy(v_hbm, kv.at[1, pl.ds(TOK, TOK)], lsem.at[1]),
        pltpu.make_async_copy(q_hbm, q_v, lsem.at[2]),
        pltpu.make_async_copy(cot_hbm, cot_v, lsem.at[3]),
        pltpu.make_async_copy(w_hbm, wf.at[d], lsem.at[4]),
    ]
    for load in loads:
        load.start()

    barrier = pltpu.get_barrier_semaphore()
    peers = [mate, after, before]
    peers += [f(n) for f in (to_x, to_y, to_z) for n in (1, 2, 3)]
    peers += [to_o(n) for n in (1, 2, 3)]
    for peer in peers:
        pl.semaphore_signal(barrier, inc=1, device_id=peer, device_id_type=MESH)

    first = s * TOK
    q_pos = first + lax.broadcasted_iota(jnp.int32, (TOK, 1), 0)
    begin = jnp.zeros((TOK, 1), jnp.int32)
    opening = len_ref[0, 0] * 0
    for n in range(DOCS):
        begin = jnp.where(q_pos >= opening, opening, begin)
        opening = opening + len_ref[0, n]
    k_pos = first - TOK + lax.broadcasted_iota(jnp.int32, (TOK, 2 * TOK), 1)
    bias[...] = jnp.where((k_pos >= begin) & (k_pos <= q_pos), 0.0, -1e30)
    gk_t[...] = jnp.zeros_like(gk_t)
    gv_t[...] = jnp.zeros_like(gv_t)

    pl.semaphore_wait(barrier, len(peers))

    prev = pl.ds(0, TOK)
    low, high = pl.ds(0, 64), pl.ds(64, 64)

    def halo(n):
        cols = pl.ds(n // 2 * DH, DH)
        source = (k_hbm, v_hbm)[n % 2]
        return HALO + n, source.at[:, cols], kv.at[n % 2, prev, cols], after

    for n in range(8):
        send(*halo(n))
    send(WX, w_hbm.at[c, low], wf.at[d, c, low], to_x(1))
    send(WX + 2, w_hbm.at[c, high], wf.at[d, c, high], to_x(3))
    send(WX + 1, w_hbm.at[c, high], wf.at[d, c, high], to_x(1))
    send(WX + 3, w_hbm.at[c, low], wf.at[d, c, low], to_x(3))
    send(WZ, w_hbm.at[c, low], wf.at[d, c, low], near)
    send(WZ + 1, w_hbm.at[c, high], wf.at[d, c, high], far)
    send(COT, cot_hbm.at[:, pl.ds(pl.multiple_of((1 - c) * 1024, 1024), 1024)], cotm, mate)

    def shard_x(i, plane):
        return plane * 4 + turn(x, (0, 3, 1, 2)[i])

    def part_x(n, i, part, relay=None):
        piece = wf.at[shard_x(i, zl), c, part]
        rc(WX + n, piece, piece, mate).wait_recv()
        if relay is not None:
            send(WX + relay[0], piece, piece, to_x(relay[1]))
        if part is low:
            send(WZ + 2 * i, piece, piece, near)
        else:
            send(WZ + 2 * i + 1, piece, piece, far)

    def to_mate(j, e):
        send(WC + j, wf.at[e, c], wf.at[e, c], mate)

    def forward_x(step):
        if step == 0:
            part_x(0, 1, low, (4, 1))
            part_x(2, 2, high, (5, 3))
        if step == 1:
            part_x(1, 1, high)
            part_x(3, 2, low)
            to_mate(0, shard_x(1, zl))
            to_mate(1, shard_x(2, zl))
        if step == 2:
            part_x(4, 3, low)
            part_x(5, 3, high)
            to_mate(2, shard_x(3, zl))

    def forward_z(i):
        e = shard_x(i, 1 - zl)
        rc(WZ + 2 * i, wf.at[e, c, low], wf.at[e, c, low], mate).wait_recv()
        rc(WZ + 2 * i + 1, wf.at[e, c, high], wf.at[e, c, high], mate).wait_recv()
        to_mate(3 + i, e)

    def from_mate(j, e):
        rc(WC + j, wf.at[e, 1 - c], wf.at[e, 1 - c], mate).wait_recv()

    for load in loads[:3]:
        load.wait()

    def head(h):
        return pl.ds(pl.multiple_of(h * DH, DH), DH)

    def fwd(k):
        for n in (2 * k, 2 * k + 1):
            rc(*halo(n)).wait_recv()
        keys, values = kv[0, :, head(k)], kv[1, :, head(k)]

        def one(g, _):
            h = k * 4 + g
            scores = dg(q_v[:, head(h)], keys, 1, 1) * SCALE + bias[...]
            e = jnp.exp(scores - jnp.max(scores, axis=-1, keepdims=True))
            p = (e * (1.0 / jnp.sum(e, axis=-1, keepdims=True))).astype(BF16)
            prob[h] = p
            att[:, head(h)] = dg(p, values, 1, 0).astype(BF16)
            return 0

        lax.fori_loop(0, 4, one, 0)
        cols = pl.ds(k * 512, 512)
        send(ATT + k, att.at[:, cols], attm.at[:, cols], mate)

    def grad_w(k):
        cols = pl.ds(k * 512, 512)
        rc(ATT + k, att.at[:, cols], attm.at[:, cols], mate).wait_recv()
        if k == 0:
            loads[3].wait()
            rc(COT, cotm, cotm, mate).wait_recv()
        for e in (2 * k, 2 * k + 1):
            own = att[:, e * 256 : (e + 1) * 256]
            other = attm[:, e * 256 : (e + 1) * 256]
            for n in range(4):
                mine = cot_v[:, pl.ds(pl.multiple_of(c * 1024 + n * 256, 256), 256)]
                part = dg(own, mine, 0, 0) + dg(other, cotm[:, n * 256 : (n + 1) * 256], 0, 0)
                part = part.astype(BF16)
                for sub in range(8):
                    rows = part[sub * 32 : (sub + 1) * 32]
                    if n < 2:
                        g_y[sub % 4, e, sub // 4, :, n * 256 : (n + 1) * 256] = rows
                    elif n == 2:
                        g_x[e % 4, e // 4, sub, :, 0:256] = rows
                    else:
                        g_x[e % 4, e // 4, sub, :, 256:384] = rows[:, 0:128]
                        g_z[sub // 4 * 2 + e // 4, e % 4, sub % 4] = rows[:, 128:256]
        both = pl.ds(2 * k, 2)
        for n in (1, 3, 2):
            send(Y1 + 3 * k + n - 1, g_y.at[turn(y, n), both], r_y1.at[n - 1, both], to_y(n))

    fwd(0)
    fwd(1)
    grad_w(0)
    forward_x(0)
    fwd(2)
    grad_w(1)
    forward_x(1)
    fwd(3)
    grad_w(2)
    forward_x(2)
    grad_w(3)
    for n in (1, 3, 2):
        send(X1 + n - 1, g_x.at[turn(x, n)], r_x1.at[n - 1], to_x(n))
        send(Z1 + n - 1, g_z.at[turn(z, n)], r_z1.at[n - 1], to_z(n))
    loads[4].wait()

    def bwd(e):
        k = lax.div(e, 2)
        weight = wf[e].reshape(256, DM)
        grad = dg(cot_v[...], weight, 1, 1).astype(BF16)
        keys, values = kv[0, :, head(k)], kv[1, :, head(k)]
        for g in range(2):
            h = 2 * e + g
            grad_h = grad[:, g * DH : (g + 1) * DH]
            delta = jnp.sum(
                grad_h.astype(F32) * att[:, head(h)].astype(F32), axis=-1, keepdims=True
            )
            p = prob[h]
            grad_s = (p.astype(F32) * (dg(grad_h, values, 1, 1) - delta)).astype(BF16)
            gq_v[:, head(h)] = (dg(grad_s, keys, 1, 0) * SCALE).astype(BF16)
            gk_t[head(k), :] += dg(q_v[:, head(h)], grad_s, 0, 0)
            gv_t[head(k), :] += dg(grad_h, p, 0, 0)

    bwd(d)
    for i in range(1, 4):
        e = shard_x(i, zl)
        if i == 1:
            forward_z(0)
        from_mate(i - 1, e)
        bwd(e)
    for i in range(4):
        e = shard_x(i, 1 - zl)
        if i < 3:
            forward_z(i + 1)
        from_mate(3 + i, e)
        bwd(e)

    back_s[0] = (gk_t[:, 0:TOK].T * SCALE).astype(BF16)
    back_s[1] = gv_t[:, 0:TOK].T.astype(BF16)
    send(BACK, back_s.at[0], back_r.at[0], before)
    send(BACK + 1, back_s.at[1], back_r.at[1], before)

    def arrived(base, dst, source):
        for n in range(3):
            rc(base + n, source, dst.at[n], mate).wait_recv()

    def total(own, got, *where):
        out = own.astype(F32)
        for n in range(3):
            out = out + got[(n, *where)].astype(F32)
        return out

    def arrived_y():
        for k in range(HK):
            both = pl.ds(2 * k, 2)
            for n in range(3):
                rc(Y1 + 3 * k + n, g_y.at[0, both], r_y1.at[n, both], mate).wait_recv()

    def project(n, _):
        cols = pl.ds(pl.multiple_of(n * 256, 256), 256)
        weight = wf[:, :, :, cols].reshape(2048, 256)
        pro_v[:, cols] = dg(att[...], weight, 1, 0).astype(BF16)
        return 0

    lax.fori_loop(0, 4, project, 0)

    arrived(Z1, r_z1, g_z.at[0])
    for x_ in range(4):
        for y_ in range(4):
            s_z[x_, y_] = total(g_z[z, x_, y_], r_z1, x_, y_).astype(BF16)
    for n in (1, 3, 2):
        send(Z2 + n - 1, s_z.at[turn(x, n)], r_z2.at[n - 1], to_x(n))

    arrived_y()
    for e in range(8):
        for zh_ in range(2):
            value = total(g_y[y, e, zh_], r_y1, e, zh_)
            s_y[zh_ * 2 + e // 4, e % 4] = value.astype(BF16)
    for n in (1, 3, 2):
        send(Y2 + n - 1, s_y.at[turn(z, n)], r_y2.at[n - 1], to_z(n))

    arrived(X1, r_x1, g_x.at[0])
    for zl_ in range(2):
        for sub in range(8):
            value = total(g_x[x, zl_, sub], r_x1, zl_, sub)
            s_x[sub % 4, sub // 4 * 2 + zl_] = value.astype(BF16)
    for n in (1, 3, 2):
        send(X2 + n - 1, s_x.at[turn(y, n)], r_x2.at[n - 1], to_y(n))

    lax.fori_loop(4, 8, project, 0)
    outs = [
        pltpu.make_async_copy(pro_v, pro_hbm, osem.at[0]),
        pltpu.make_async_copy(gq_v, gq_hbm, osem.at[1]),
    ]
    for out in outs:
        out.start()

    arrived(Z2, r_z2, s_z.at[0])
    for y_ in range(4):
        s_z2[y_] = total(s_z[x, y_], r_z2, y_).astype(BF16)
    for n in (1, 3, 2):
        send(Z3 + n - 1, s_z2.at[turn(y, n)], r_z3.at[n - 1], to_y(n))
    arrived(Y2, r_y2, s_y.at[0])
    for x_ in range(4):
        s_y2[x_] = total(s_y[z, x_], r_y2, x_).astype(BF16)
    for n in (1, 3, 2):
        send(Y3 + n - 1, s_y2.at[turn(x, n)], r_y3.at[n - 1], to_x(n))
    arrived(X2, r_x2, s_x.at[0])
    for z_ in range(4):
        s_x2[z_] = total(s_x[y, z_], r_x2, z_).astype(BF16)
    for n in (1, 3, 2):
        send(X3 + n - 1, s_x2.at[turn(z, n)], r_x3.at[n - 1], to_z(n))

    factor = 1.0 / math.sqrt(TOTAL)
    piece_of = zh * 4 + y

    def gather(chunk):
        piece = agb.at[chunk, c, piece_of]
        for n in range(7):
            send(AG + 7 * chunk + n, piece, piece, to_y(n + 1) if n < 3 else to_o(n - 3))

    def origin(n):
        return zh * 4 + turn(y, 3 - n) if n < 3 else (1 - zh) * 4 + turn(y, 7 - n)

    def gathered(chunk):
        for n in range(7):
            piece = agb.at[chunk, c, origin(n)]
            rc(AG + 7 * chunk + n, piece, piece, mate).wait_recv()
        send(AGC + chunk, agb.at[chunk, c], agb.at[chunk, c], mate)

    def finished(chunk):
        half = agb.at[chunk, 1 - c]
        rc(AGC + chunk, half, half, mate).wait_recv()
        outs.append(pltpu.make_async_copy(agb.at[chunk], gw_hbm.at[chunk], osem.at[4 + chunk]))
        outs[-1].start()

    arrived(Y3, r_y3, s_y2.at[0])
    agb[0, c, piece_of] = (total(s_y2[x], r_y3) * factor).astype(BF16)
    gather(0)
    arrived(Z3, r_z3, s_z2.at[0])
    agb[1, c, piece_of, :, 384:512] = (total(s_z2[y], r_z3) * factor).astype(BF16)
    arrived(X3, r_x3, s_x2.at[0])
    agb[1, c, piece_of, :, 0:384] = (total(s_x2[z], r_x3) * factor).astype(BF16)
    gather(1)

    rc(BACK, back_s.at[0], back_r.at[0], before).wait_recv()
    rc(BACK + 1, back_s.at[1], back_r.at[1], before).wait_recv()
    gkv_v[0] = (gk_t[:, TOK : 2 * TOK].T * SCALE + back_r[0].astype(F32)).astype(BF16)
    gkv_v[1] = (gv_t[:, TOK : 2 * TOK].T + back_r[1].astype(F32)).astype(BF16)
    for n, out in enumerate((gk_hbm, gv_hbm)):
        outs.append(pltpu.make_async_copy(gkv_v.at[n], out, osem.at[2 + n]))
        outs[-1].start()

    gathered(0)
    gathered(1)
    finished(0)
    finished(1)
    for copy in sent:
        copy.wait_send()
    for out in outs:
        out.wait()


def finish(pro, gq, gk, gv, gw, pro_o, gq_o, gk_o, gv_o, gw_o, wide, sem):
    pairs = ((pro, pro_o), (gq, gq_o), (gk, gk_o), (gv, gv_o))
    copies = [pltpu.make_async_copy(a, b, sem.at[n]) for n, (a, b) in enumerate(pairs)]
    for copy in copies:
        copy.start()
    for chunk in range(2):
        for half in range(2):
            at = half * 1024 + chunk * 512
            wide[:, at : at + 512] = gw[chunk, half].reshape(TOK, 512).astype(F32)
    copies.append(pltpu.make_async_copy(wide, gw_o, sem.at[4]))
    copies[4].start()
    for copy in copies:
        copy.wait()


def body(queries, key_heads, value_heads, doc_lengths, out_weight, cotangent):
    anywhere = pl.BlockSpec(memory_space=pl.ANY)
    shapes = [
        ((TOK, 2048), BF16),
        ((TOK, 2048), BF16),
        ((2, 512, 512), BF16),
        ((8, 2, 128, 2048), BF16),
        ((TOK, 1024), BF16),
        ((TOK, 2048), BF16),
        ((TOK, 2048), BF16),
        ((HQ, TOK, 512), BF16),
        ((TOK, 512), F32),
        ((4, 8, 2, 32, 512), BF16),
        ((3, 8, 2, 32, 512), BF16),
        ((4, 4, 32, 512), BF16),
        ((3, 4, 32, 512), BF16),
        ((4, 32, 512), BF16),
        ((3, 32, 512), BF16),
        ((4, 2, 8, 32, 384), BF16),
        ((3, 2, 8, 32, 384), BF16),
        ((4, 4, 32, 384), BF16),
        ((3, 4, 32, 384), BF16),
        ((4, 32, 384), BF16),
        ((3, 32, 384), BF16),
        ((4, 4, 4, 32, 128), BF16),
        ((3, 4, 4, 32, 128), BF16),
        ((4, 4, 32, 128), BF16),
        ((3, 4, 32, 128), BF16),
        ((4, 32, 128), BF16),
        ((3, 32, 128), BF16),
        ((2, 2, 8, 32, 512), BF16),
        ((512, 512), F32),
        ((512, 512), F32),
        ((2, TOK, 512), BF16),
        ((2, TOK, 512), BF16),
        ((TOK, 2048), BF16),
        ((TOK, 2048), BF16),
        ((2, TOK, 512), BF16),
    ]
    scratch = [pltpu.VMEM(shape, dtype) for shape, dtype in shapes]
    scratch += [pltpu.SemaphoreType.DMA((n,)) for n in (COPIES, COPIES, 5, 6)]
    results = [
        jax.ShapeDtypeStruct((TOK, 2048), BF16),
        jax.ShapeDtypeStruct((TOK, 2048), BF16),
        jax.ShapeDtypeStruct((TOK, 512), BF16),
        jax.ShapeDtypeStruct((TOK, 512), BF16),
    ]
    outs = pl.pallas_call(
        kernel,
        out_shape=[*results, jax.ShapeDtypeStruct((2, 2, 8, 32, 512), BF16)],
        in_specs=[pl.BlockSpec(memory_space=pltpu.SMEM)] + [anywhere] * 5,
        out_specs=[anywhere] * 5,
        scratch_shapes=scratch,
        compiler_params=pltpu.CompilerParams(
            collective_id=0, has_side_effects=True, vmem_limit_bytes=56 << 20
        ),
        cost_estimate=pl.CostEstimate(
            flops=10_000_000_000, bytes_accessed=12_000_000, transcendentals=2_000_000
        ),
    )(
        doc_lengths,
        queries[0],
        key_heads[0],
        value_heads[0],
        out_weight.reshape(2, 128, DM),
        cotangent[0],
    )
    outs = pl.pallas_call(
        finish,
        out_shape=[*results, jax.ShapeDtypeStruct((TOK, 2048), F32)],
        in_specs=[pl.BlockSpec(memory_space=pltpu.VMEM)] * 5,
        out_specs=[anywhere] * 5,
        scratch_shapes=[pltpu.VMEM((TOK, 2048), F32), pltpu.SemaphoreType.DMA((5,))],
    )(*outs)
    return (*(out[None] for out in outs[:4]), outs[4])


def solution(mesh):
    tokens = P("dp", "seq", None)
    rows = P("dp", None)
    return jax.shard_map(
        body,
        mesh=mesh,
        in_specs=(tokens, tokens, tokens, rows, rows, tokens),
        out_specs=(tokens, tokens, tokens, tokens, rows),
        check_vma=False,
    )
```

```python
import math

import jax
import jax.numpy as jnp
from jax import lax
from jax.experimental import pallas as pl
from jax.experimental.pallas import tpu as pltpu
from jax.sharding import PartitionSpec as P

HQ = 16
HK = 4
DH = 128
DM = 2048
TOK = 256
DOCS = 32
TOTAL = 32768
SCALE = 1.0 / math.sqrt(DH)
F32 = jnp.float32
BF16 = jnp.bfloat16
MESH = pl.DeviceIdType.MESH

HALO = 0
WX = HALO + 8
WZ = WX + 6
WC = WZ + 8
COT = WC + 7
ATT = COT + 1
Y1 = ATT + 4
X1 = Y1 + 24
Z1 = X1 + 6
Y2 = Z1 + 6
X2 = Y2 + 3
Z2 = X2 + 3
Y3 = Z2 + 3
X3 = Y3 + 3
Z3 = X3 + 3
BACK = Z3 + 3
AG = BACK + 2
AGC = AG + 14
COPIES = AGC + 2


def dg(a, b, ca, cb):
    return lax.dot_general(a, b, (((ca,), (cb,)), ((), ())), preferred_element_type=F32)


def kernel(
    len_ref, q_hbm, k_hbm, v_hbm, w_hbm, cot_hbm,
    pro_hbm, gq_hbm, gk_hbm, gv_hbm, gw_hbm,
    q_v, cot_v, kv, wf, cotm, att, attm, prob, bias,
    g_y, r_y1, s_y, r_y2, s_y2, r_y3,
    g_x, r_x1, s_x, r_x2, s_x2, r_x3,
    g_z, r_z1, s_z, r_z2, s_z2, r_z3,
    agb, gk_t, gv_t, back_s, back_r,
    pro_v, gq_v, gkv_v,
    ssem, rsem, lsem, osem,
):
    s = lax.axis_index("seq")
    d = lax.axis_index("dp")
    zh = lax.div(s, 8)
    y = lax.rem(lax.div(s, 2), 4)
    c = lax.rem(s, 2)
    zl = lax.div(d, 4)
    x = lax.rem(d, 4)
    z = zh * 2 + zl

    def at(zh_, y_, c_, zl_, x_):
        return {"seq": zh_ * 8 + y_ * 2 + c_, "dp": zl_ * 4 + x_}

    def turn(v, n):
        return lax.rem(v + n, 4)

    def to_x(n):
        return at(zh, y, c, zl, turn(x, n))

    def to_y(n):
        return at(zh, turn(y, n), c, zl, x)

    def to_z(n):
        zz = turn(z, n)
        return at(lax.div(zz, 2), y, c, lax.rem(zz, 2), x)

    def to_o(n):
        return at(1 - zh, turn(y, n), c, zl, x)

    mate = at(zh, y, 1 - c, zl, x)
    near = at(zh, y, c, 1 - zl, x)
    far = at(1 - zh, y, c, 1 - zl, x)
    after = {"seq": lax.rem(s + 1, 16), "dp": d}
    before = {"seq": lax.rem(s + 15, 16), "dp": d}

    def rc(n, src, dst, to):
        return pltpu.make_async_remote_copy(
            src_ref=src, dst_ref=dst, send_sem=ssem.at[n], recv_sem=rsem.at[n],
            device_id=to, device_id_type=MESH,
        )

    sent = []

    def send(n, src, dst, to):
        copy = rc(n, src, dst, to)
        copy.start()
        sent.append(copy)

    loads = [
        pltpu.make_async_copy(k_hbm, kv.at[0, pl.ds(TOK, TOK)], lsem.at[0]),
        pltpu.make_async_copy(v_hbm, kv.at[1, pl.ds(TOK, TOK)], lsem.at[1]),
        pltpu.make_async_copy(q_hbm, q_v, lsem.at[2]),
        pltpu.make_async_copy(cot_hbm, cot_v, lsem.at[3]),
        pltpu.make_async_copy(w_hbm, wf.at[d], lsem.at[4]),
    ]
    for load in loads:
        load.start()

    barrier = pltpu.get_barrier_semaphore()
    peers = [mate, after, before]
    peers += [f(n) for f in (to_x, to_y, to_z) for n in (1, 2, 3)]
    peers += [to_o(n) for n in (1, 2, 3)]
    for peer in peers:
        pl.semaphore_signal(barrier, inc=1, device_id=peer, device_id_type=MESH)

    first = s * TOK
    q_pos = first + lax.broadcasted_iota(jnp.int32, (TOK, 1), 0)
    begin = jnp.zeros((TOK, 1), jnp.int32)
    opening = len_ref[0, 0] * 0
    for n in range(DOCS):
        begin = jnp.where(q_pos >= opening, opening, begin)
        opening = opening + len_ref[0, n]
    k_pos = first - TOK + lax.broadcasted_iota(jnp.int32, (TOK, 2 * TOK), 1)
    bias[...] = jnp.where((k_pos >= begin) & (k_pos <= q_pos), 0.0, -1e30)
    gk_t[...] = jnp.zeros_like(gk_t)
    gv_t[...] = jnp.zeros_like(gv_t)

    pl.semaphore_wait(barrier, len(peers))

    prev = pl.ds(0, TOK)
    low, high = pl.ds(0, 64), pl.ds(64, 64)

    def halo(n):
        cols = pl.ds(n // 2 * DH, DH)
        source = (k_hbm, v_hbm)[n % 2]
        return HALO + n, source.at[:, cols], kv.at[n % 2, prev, cols], after

    for n in range(8):
        send(*halo(n))
    send(WX, w_hbm.at[c, low], wf.at[d, c, low], to_x(1))
    send(WX + 2, w_hbm.at[c, high], wf.at[d, c, high], to_x(3))
    send(WX + 1, w_hbm.at[c, high], wf.at[d, c, high], to_x(1))
    send(WX + 3, w_hbm.at[c, low], wf.at[d, c, low], to_x(3))
    send(WZ, w_hbm.at[c, low], wf.at[d, c, low], near)
    send(WZ + 1, w_hbm.at[c, high], wf.at[d, c, high], far)
    send(COT, cot_hbm.at[:, pl.ds(pl.multiple_of((1 - c) * 1024, 1024), 1024)], cotm, mate)

    def shard_x(i, plane):
        return plane * 4 + turn(x, (0, 3, 1, 2)[i])

    def part_x(n, i, part, relay=None):
        piece = wf.at[shard_x(i, zl), c, part]
        rc(WX + n, piece, piece, mate).wait_recv()
        if relay is not None:
            send(WX + relay[0], piece, piece, to_x(relay[1]))
        if part is low:
            send(WZ + 2 * i, piece, piece, near)
        else:
            send(WZ + 2 * i + 1, piece, piece, far)

    def to_mate(j, e):
        send(WC + j, wf.at[e, c], wf.at[e, c], mate)

    def forward_x(step):
        if step == 0:
            part_x(0, 1, low, (4, 1))
            part_x(2, 2, high, (5, 3))
        if step == 1:
            part_x(1, 1, high)
            part_x(3, 2, low)
            to_mate(0, shard_x(1, zl))
            to_mate(1, shard_x(2, zl))
        if step == 2:
            part_x(4, 3, low)
            part_x(5, 3, high)
            to_mate(2, shard_x(3, zl))

    def forward_z(i):
        e = shard_x(i, 1 - zl)
        rc(WZ + 2 * i, wf.at[e, c, low], wf.at[e, c, low], mate).wait_recv()
        rc(WZ + 2 * i + 1, wf.at[e, c, high], wf.at[e, c, high], mate).wait_recv()
        to_mate(3 + i, e)

    def from_mate(j, e):
        rc(WC + j, wf.at[e, 1 - c], wf.at[e, 1 - c], mate).wait_recv()

    for load in loads[:3]:
        load.wait()

    class Ring:
        def __init__(self, base, v, to, piece, slot):
            self.base, self.v, self.piece, self.slot = base, v, piece, slot
            self.up, self.down = to(1), to(3)

        def start(self):
            v, piece, slot = self.v, self.piece, self.slot
            send(self.base, piece(turn(v, 2), 0), slot(0), self.up)
            send(self.base + 1, piece(turn(v, 2), 1), slot(1), self.down)
            send(self.base + 2, piece(turn(v, 1), 1), slot(2), self.up)
            send(self.base + 3, piece(turn(v, 3), 0), slot(3), self.down)

        def relay(self):
            for part, n, to in ((0, 1, self.up), (1, 3, self.down)):
                mid, got = self.piece(turn(self.v, n), part), self.slot(part)
                rc(self.base + part, got, got, mate).wait_recv()
                mid[...] = (mid[...].astype(F32) + got[...].astype(F32)).astype(BF16)
                send(self.base + 4 + part, mid, self.slot(4 + part), to)

        def wait(self):
            for n in range(2, 6):
                rc(self.base + n, self.slot(n), self.slot(n), mate).wait_recv()

    def ring_of_y(k):
        return Ring(
            Y1 + 6 * k, y, to_y, lambda to, part: g_y.at[to, 2 * k + part], lambda n: r_y1.at[n, k]
        )

    ring_y = [ring_of_y(k) for k in range(HK)]
    ring_x = Ring(X1, x, to_x, lambda to, part: g_x.at[to, part], lambda n: r_x1.at[n])
    ring_z = Ring(Z1, z, to_z, lambda to, part: g_z.at[to, part], lambda n: r_z1.at[n])

    def head(h):
        return pl.ds(pl.multiple_of(h * DH, DH), DH)

    def fwd(k):
        for n in (2 * k, 2 * k + 1):
            rc(*halo(n)).wait_recv()
        keys, values = kv[0, :, head(k)], kv[1, :, head(k)]

        def one(g, _):
            h = k * 4 + g
            scores = dg(q_v[:, head(h)], keys, 1, 1) * SCALE + bias[...]
            e = jnp.exp(scores - jnp.max(scores, axis=-1, keepdims=True))
            p = (e * (1.0 / jnp.sum(e, axis=-1, keepdims=True))).astype(BF16)
            prob[h] = p
            att[:, head(h)] = dg(p, values, 1, 0).astype(BF16)
            return 0

        lax.fori_loop(0, 4, one, 0, unroll=True)
        cols = pl.ds(k * 512, 512)
        send(ATT + k, att.at[:, cols], attm.at[:, cols], mate)

    def grad_w(k):
        cols = pl.ds(k * 512, 512)
        rc(ATT + k, att.at[:, cols], attm.at[:, cols], mate).wait_recv()
        if k == 0:
            loads[3].wait()
            rc(COT, cotm, cotm, mate).wait_recv()
        for e in (2 * k, 2 * k + 1):
            own = att[:, e * 256 : (e + 1) * 256]
            other = attm[:, e * 256 : (e + 1) * 256]
            for n in range(4):
                mine = cot_v[:, pl.ds(pl.multiple_of(c * 1024 + n * 256, 256), 256)]
                part = dg(own, mine, 0, 0) + dg(other, cotm[:, n * 256 : (n + 1) * 256], 0, 0)
                part = part.astype(BF16)
                for sub in range(8):
                    rows = part[sub * 32 : (sub + 1) * 32]
                    if n < 2:
                        g_y[sub % 4, e, sub // 4, :, n * 256 : (n + 1) * 256] = rows
                    elif n == 2:
                        g_x[e % 4, e // 4, sub, :, 0:256] = rows
                    else:
                        g_x[e % 4, e // 4, sub, :, 256:384] = rows[:, 0:128]
                        g_z[sub // 4 * 2 + e // 4, e % 4 // 2, e % 2, sub % 4] = rows[:, 128:256]
    fwd(0)
    fwd(1)
    grad_w(0)
    ring_y[0].start()
    fwd(2)
    forward_x(0)
    grad_w(1)
    ring_y[1].start()
    ring_y[0].relay()
    fwd(3)
    grad_w(2)
    ring_y[2].start()
    ring_y[1].relay()
    forward_x(1)
    grad_w(3)
    ring_y[3].start()
    ring_x.start()
    ring_z.start()
    ring_y[2].relay()
    forward_z(0)
    loads[4].wait()

    def bwd(e):
        k = lax.div(e, 2)
        weight = wf[e].reshape(256, DM)
        grad = dg(cot_v[...], weight, 1, 1).astype(BF16)
        keys, values = kv[0, :, head(k)], kv[1, :, head(k)]
        for g in range(2):
            h = 2 * e + g
            grad_h = grad[:, g * DH : (g + 1) * DH]
            delta = jnp.sum(
                grad_h.astype(F32) * att[:, head(h)].astype(F32), axis=-1, keepdims=True
            )
            p = prob[h]
            grad_s = (p.astype(F32) * (dg(grad_h, values, 1, 1) - delta)).astype(BF16)
            gq_v[:, head(h)] = (dg(grad_s, keys, 1, 0) * SCALE).astype(BF16)
            gk_t[head(k), :] += dg(q_v[:, head(h)], grad_s, 0, 0)
            gv_t[head(k), :] += dg(grad_h, p, 0, 0)

    def bwd_x(i):
        e = shard_x(i, zl)
        from_mate(i - 1, e)
        bwd(e)

    def bwd_z(i):
        e = shard_x(i, 1 - zl)
        from_mate(3 + i, e)
        bwd(e)

    def arrived(base, dst, source):
        for n in range(3):
            rc(base + n, source, dst.at[n], mate).wait_recv()

    def total(own, got, *where):
        out = own.astype(F32)
        for n in range(3):
            out = out + got[(n, *where)].astype(F32)
        return out

    def settled(own, got, part, *where):
        one, two = ((3, 4), (2, 5))[part]
        return own.astype(F32) + got[(one, *where)].astype(F32) + got[(two, *where)].astype(F32)

    def project(n, _):
        cols = pl.ds(n * 256, 256)
        weight = wf[:, :, :, cols].reshape(2048, 256)
        pro_v[:, cols] = dg(att[...], weight, 1, 0).astype(BF16)
        return 0

    def sum_z():
        ring_z.wait()
        for x_ in range(4):
            for y_ in range(4):
                where = (x_ % 2, y_)
                value = settled(g_z[(z, x_ // 2, *where)], r_z1, x_ // 2, *where)
                s_z[x_, y_] = value.astype(BF16)
        for n in (1, 3, 2):
            send(Z2 + n - 1, s_z.at[turn(x, n)], r_z2.at[n - 1], to_x(n))

    def sum_y():
        for ring in ring_y:
            ring.wait()
        for e in range(8):
            for zh_ in range(2):
                value = settled(g_y[y, e, zh_], r_y1, e % 2, e // 2, zh_)
                s_y[zh_ * 2 + e // 4, e % 4] = value.astype(BF16)
        for n in (1, 3, 2):
            send(Y2 + n - 1, s_y.at[turn(z, n)], r_y2.at[n - 1], to_z(n))

    def sum_x():
        ring_x.wait()
        for zl_ in range(2):
            for sub in range(8):
                value = settled(g_x[x, zl_, sub], r_x1, zl_, sub)
                s_x[sub % 4, sub // 4 * 2 + zl_] = value.astype(BF16)
        for n in (1, 3, 2):
            send(X2 + n - 1, s_x.at[turn(y, n)], r_x2.at[n - 1], to_y(n))

    bwd(d)
    forward_x(2)
    bwd_x(1)
    bwd_x(2)
    ring_y[3].relay()
    forward_z(1)
    bwd_z(0)
    forward_z(2)
    bwd_x(3)
    ring_x.relay()
    ring_z.relay()
    bwd_z(1)
    sum_y()
    bwd_z(2)
    forward_z(3)
    sum_z()
    sum_x()
    bwd_z(3)

    back_s[0] = (gk_t[:, 0:TOK].T * SCALE).astype(BF16)
    back_s[1] = gv_t[:, 0:TOK].T.astype(BF16)
    send(BACK, back_s.at[0], back_r.at[0], before)
    send(BACK + 1, back_s.at[1], back_r.at[1], before)

    for n in range(6):
        project(n, 0)
    arrived(Y2, r_y2, s_y.at[0])
    for x_ in range(4):
        s_y2[x_] = total(s_y[z, x_], r_y2, x_).astype(BF16)
    for n in (1, 3, 2):
        send(Y3 + n - 1, s_y2.at[turn(x, n)], r_y3.at[n - 1], to_x(n))
    arrived(Z2, r_z2, s_z.at[0])
    for y_ in range(4):
        s_z2[y_] = total(s_z[x, y_], r_z2, y_).astype(BF16)
    for n in (1, 3, 2):
        send(Z3 + n - 1, s_z2.at[turn(y, n)], r_z3.at[n - 1], to_y(n))
    arrived(X2, r_x2, s_x.at[0])
    for z_ in range(4):
        s_x2[z_] = total(s_x[y, z_], r_x2, z_).astype(BF16)
    for n in (1, 3, 2):
        send(X3 + n - 1, s_x2.at[turn(z, n)], r_x3.at[n - 1], to_z(n))
    for n in range(6, 8):
        project(n, 0)
    outs = [
        pltpu.make_async_copy(pro_v, pro_hbm, osem.at[0]),
        pltpu.make_async_copy(gq_v, gq_hbm, osem.at[1]),
    ]
    for out in outs:
        out.start()


    factor = 1.0 / math.sqrt(TOTAL)
    piece_of = zh * 4 + y

    def gather(chunk):
        piece = agb.at[chunk, c, piece_of]
        for n in range(7):
            send(AG + 7 * chunk + n, piece, piece, to_y(n + 1) if n < 3 else to_o(n - 3))

    def origin(n):
        return zh * 4 + turn(y, 3 - n) if n < 3 else (1 - zh) * 4 + turn(y, 7 - n)

    def gathered(chunk):
        for n in range(7):
            piece = agb.at[chunk, c, origin(n)]
            rc(AG + 7 * chunk + n, piece, piece, mate).wait_recv()
        send(AGC + chunk, agb.at[chunk, c], agb.at[chunk, c], mate)

    def finished(chunk):
        half = agb.at[chunk, 1 - c]
        rc(AGC + chunk, half, half, mate).wait_recv()
        outs.append(pltpu.make_async_copy(agb.at[chunk], gw_hbm.at[chunk], osem.at[4 + chunk]))
        outs[-1].start()

    arrived(Y3, r_y3, s_y2.at[0])
    agb[0, c, piece_of] = (total(s_y2[x], r_y3) * factor).astype(BF16)
    gather(0)
    arrived(Z3, r_z3, s_z2.at[0])
    agb[1, c, piece_of, :, 384:512] = (total(s_z2[y], r_z3) * factor).astype(BF16)
    arrived(X3, r_x3, s_x2.at[0])
    agb[1, c, piece_of, :, 0:384] = (total(s_x2[z], r_x3) * factor).astype(BF16)
    gather(1)

    rc(BACK, back_s.at[0], back_r.at[0], before).wait_recv()
    rc(BACK + 1, back_s.at[1], back_r.at[1], before).wait_recv()
    gkv_v[0] = (gk_t[:, TOK : 2 * TOK].T * SCALE + back_r[0].astype(F32)).astype(BF16)
    gkv_v[1] = (gv_t[:, TOK : 2 * TOK].T + back_r[1].astype(F32)).astype(BF16)
    for n, out in enumerate((gk_hbm, gv_hbm)):
        outs.append(pltpu.make_async_copy(gkv_v.at[n], out, osem.at[2 + n]))
        outs[-1].start()

    gathered(0)
    gathered(1)
    finished(0)
    finished(1)
    for copy in sent:
        copy.wait_send()
    for out in outs:
        out.wait()


def finish(pro, gq, gk, gv, gw, pro_o, gq_o, gk_o, gv_o, gw_o, wide, sem):
    pairs = ((pro, pro_o), (gq, gq_o), (gk, gk_o), (gv, gv_o))
    copies = [pltpu.make_async_copy(a, b, sem.at[n]) for n, (a, b) in enumerate(pairs)]
    for copy in copies:
        copy.start()
    for chunk in range(2):
        for half in range(2):
            at = half * 1024 + chunk * 512
            wide[:, at : at + 512] = gw[chunk, half].reshape(TOK, 512).astype(F32)
    copies.append(pltpu.make_async_copy(wide, gw_o, sem.at[4]))
    copies[4].start()
    for copy in copies:
        copy.wait()


def body(queries, key_heads, value_heads, doc_lengths, out_weight, cotangent):
    anywhere = pl.BlockSpec(memory_space=pl.ANY)
    shapes = [
        ((TOK, 2048), BF16),
        ((TOK, 2048), BF16),
        ((2, 512, 512), BF16),
        ((8, 2, 128, 2048), BF16),
        ((TOK, 1024), BF16),
        ((TOK, 2048), BF16),
        ((TOK, 2048), BF16),
        ((HQ, TOK, 512), BF16),
        ((TOK, 512), F32),
        ((4, 8, 2, 32, 512), BF16),
        ((6, 4, 2, 32, 512), BF16),
        ((4, 4, 32, 512), BF16),
        ((3, 4, 32, 512), BF16),
        ((4, 32, 512), BF16),
        ((3, 32, 512), BF16),
        ((4, 2, 8, 32, 384), BF16),
        ((6, 8, 32, 384), BF16),
        ((4, 4, 32, 384), BF16),
        ((3, 4, 32, 384), BF16),
        ((4, 32, 384), BF16),
        ((3, 32, 384), BF16),
        ((4, 2, 2, 4, 32, 128), BF16),
        ((6, 2, 4, 32, 128), BF16),
        ((4, 4, 32, 128), BF16),
        ((3, 4, 32, 128), BF16),
        ((4, 32, 128), BF16),
        ((3, 32, 128), BF16),
        ((2, 2, 8, 32, 512), BF16),
        ((512, 512), F32),
        ((512, 512), F32),
        ((2, TOK, 512), BF16),
        ((2, TOK, 512), BF16),
        ((TOK, 2048), BF16),
        ((TOK, 2048), BF16),
        ((2, TOK, 512), BF16),
    ]
    scratch = [pltpu.VMEM(shape, dtype) for shape, dtype in shapes]
    scratch += [pltpu.SemaphoreType.DMA((n,)) for n in (COPIES, COPIES, 5, 6)]
    results = [
        jax.ShapeDtypeStruct((TOK, 2048), BF16),
        jax.ShapeDtypeStruct((TOK, 2048), BF16),
        jax.ShapeDtypeStruct((TOK, 512), BF16),
        jax.ShapeDtypeStruct((TOK, 512), BF16),
    ]
    outs = pl.pallas_call(
        kernel,
        out_shape=[*results, jax.ShapeDtypeStruct((2, 2, 8, 32, 512), BF16)],
        in_specs=[pl.BlockSpec(memory_space=pltpu.SMEM)] + [anywhere] * 5,
        out_specs=[anywhere] * 5,
        scratch_shapes=scratch,
        compiler_params=pltpu.CompilerParams(
            collective_id=0, has_side_effects=True, vmem_limit_bytes=56 << 20
        ),
        cost_estimate=pl.CostEstimate(
            flops=10_000_000_000, bytes_accessed=12_000_000, transcendentals=2_000_000
        ),
    )(
        doc_lengths,
        queries[0],
        key_heads[0],
        value_heads[0],
        out_weight.reshape(2, 128, DM),
        cotangent[0],
    )
    outs = pl.pallas_call(
        finish,
        out_shape=[*results, jax.ShapeDtypeStruct((TOK, 2048), F32)],
        in_specs=[pl.BlockSpec(memory_space=pltpu.VMEM)] * 5,
        out_specs=[anywhere] * 5,
        scratch_shapes=[pltpu.VMEM((TOK, 2048), F32), pltpu.SemaphoreType.DMA((5,))],
    )(*outs)
    return (*(out[None] for out in outs[:4]), outs[4])


def solution(mesh):
    tokens = P("dp", "seq", None)
    rows = P("dp", None)
    return jax.shard_map(
        body,
        mesh=mesh,
        in_specs=(tokens, tokens, tokens, rows, rows, tokens),
        out_specs=(tokens, tokens, tokens, tokens, rows),
        check_vma=False,
    )
```

```python
import math

import jax
import jax.numpy as jnp
from jax import lax
from jax.experimental import pallas as pl
from jax.experimental.pallas import tpu as pltpu
from jax.sharding import PartitionSpec as P

HQ = 16
HK = 4
DH = 128
DM = 2048
TOK = 256
DOCS = 32
TOTAL = 32768
SCALE = 1.0 / math.sqrt(DH)
F32 = jnp.float32
BF16 = jnp.bfloat16
MESH = pl.DeviceIdType.MESH

HALO = 0
WX = HALO + 8
WZ = WX + 6
WC = WZ + 8
COT = WC + 7
ATT = COT + 1
Y1 = ATT + 4
X1 = Y1 + 24
Z1 = X1 + 6
Y2 = Z1 + 6
X2 = Y2 + 3
Z2 = X2 + 3
Y3 = Z2 + 3
X3 = Y3 + 3
Z3 = X3 + 3
BACK = Z3 + 3
AG = BACK + 4
AGC = AG + 14
COPIES = AGC + 4


def dg(a, b, ca, cb):
    return lax.dot_general(a, b, (((ca,), (cb,)), ((), ())), preferred_element_type=F32)


def kernel(
    len_ref, q_hbm, k_hbm, v_hbm, w_hbm, cot_hbm,
    pro_hbm, gq_hbm, gk_hbm, gv_hbm, gw_hbm,
    q_v, cot_v, kv, wf, cotm, att, attm, prob, bias,
    g_y, r_y1, s_y, r_y2, s_y2, r_y3,
    g_x, r_x1, s_x, r_x2, s_x2, r_x3,
    g_z, r_z1, s_z, r_z2, s_z2, r_z3,
    agb, gk_t, gv_t, back_s, back_r,
    pro_v, gq_v, gkv_v,
    ssem, rsem, lsem, osem,
):
    s = lax.axis_index("seq")
    d = lax.axis_index("dp")
    zh = lax.div(s, 8)
    y = lax.rem(lax.div(s, 2), 4)
    c = lax.rem(s, 2)
    zl = lax.div(d, 4)
    x = lax.rem(d, 4)
    z = zh * 2 + zl

    def at(zh_, y_, c_, zl_, x_):
        return {"seq": zh_ * 8 + y_ * 2 + c_, "dp": zl_ * 4 + x_}

    def turn(v, n):
        return lax.rem(v + n, 4)

    def to_x(n):
        return at(zh, y, c, zl, turn(x, n))

    def to_y(n):
        return at(zh, turn(y, n), c, zl, x)

    def to_z(n):
        zz = turn(z, n)
        return at(lax.div(zz, 2), y, c, lax.rem(zz, 2), x)

    def to_o(n):
        return at(1 - zh, turn(y, n), c, zl, x)

    mate = at(zh, y, 1 - c, zl, x)
    near = at(zh, y, c, 1 - zl, x)
    far = at(1 - zh, y, c, 1 - zl, x)
    after = {"seq": lax.rem(s + 1, 16), "dp": d}
    before = {"seq": lax.rem(s + 15, 16), "dp": d}

    def rc(n, src, dst, to):
        return pltpu.make_async_remote_copy(
            src_ref=src, dst_ref=dst, send_sem=ssem.at[n], recv_sem=rsem.at[n],
            device_id=to, device_id_type=MESH,
        )

    sent = []

    def send(n, src, dst, to):
        copy = rc(n, src, dst, to)
        copy.start()
        sent.append(copy)

    loads = [
        pltpu.make_async_copy(k_hbm, kv.at[0, pl.ds(TOK, TOK)], lsem.at[0]),
        pltpu.make_async_copy(v_hbm, kv.at[1, pl.ds(TOK, TOK)], lsem.at[1]),
        pltpu.make_async_copy(q_hbm, q_v, lsem.at[2]),
        pltpu.make_async_copy(cot_hbm, cot_v, lsem.at[3]),
        pltpu.make_async_copy(w_hbm, wf.at[d], lsem.at[4]),
    ]
    for load in loads:
        load.start()

    barrier = pltpu.get_barrier_semaphore()
    peers = [mate, after, before]
    peers += [f(n) for f in (to_x, to_y, to_z) for n in (1, 2, 3)]
    peers += [to_o(n) for n in (1, 2, 3)]
    for peer in peers:
        pl.semaphore_signal(barrier, inc=1, device_id=peer, device_id_type=MESH)

    first = s * TOK
    q_pos = first + lax.broadcasted_iota(jnp.int32, (TOK, 1), 0)
    begin = jnp.zeros((TOK, 1), jnp.int32)
    opening = len_ref[0, 0] * 0
    for n in range(DOCS):
        begin = jnp.where(q_pos >= opening, opening, begin)
        opening = opening + len_ref[0, n]
    k_pos = first - TOK + lax.broadcasted_iota(jnp.int32, (TOK, 2 * TOK), 1)
    bias[...] = jnp.where((k_pos >= begin) & (k_pos <= q_pos), 0.0, -1e30)
    gk_t[...] = jnp.zeros_like(gk_t)
    gv_t[...] = jnp.zeros_like(gv_t)

    pl.semaphore_wait(barrier, len(peers))

    prev = pl.ds(0, TOK)
    low, high = pl.ds(0, 64), pl.ds(64, 64)

    def halo(n):
        cols = pl.ds(n // 2 * DH, DH)
        source = (k_hbm, v_hbm)[n % 2]
        return HALO + n, source.at[:, cols], kv.at[n % 2, prev, cols], after

    for n in range(8):
        send(*halo(n))
    send(WX, w_hbm.at[c, low], wf.at[d, c, low], to_x(1))
    send(WX + 2, w_hbm.at[c, high], wf.at[d, c, high], to_x(3))
    send(WX + 1, w_hbm.at[c, high], wf.at[d, c, high], to_x(1))
    send(WX + 3, w_hbm.at[c, low], wf.at[d, c, low], to_x(3))
    send(WZ, w_hbm.at[c, low], wf.at[d, c, low], near)
    send(WZ + 1, w_hbm.at[c, high], wf.at[d, c, high], far)
    send(COT, cot_hbm.at[:, pl.ds(pl.multiple_of((1 - c) * 1024, 1024), 1024)], cotm, mate)

    def shard_x(i, plane):
        return plane * 4 + turn(x, (0, 3, 1, 2)[i])

    def part_x(n, i, part, relay=None):
        piece = wf.at[shard_x(i, zl), c, part]
        rc(WX + n, piece, piece, mate).wait_recv()
        if relay is not None:
            send(WX + relay[0], piece, piece, to_x(relay[1]))
        if part is low:
            send(WZ + 2 * i, piece, piece, near)
        else:
            send(WZ + 2 * i + 1, piece, piece, far)

    def to_mate(j, e):
        send(WC + j, wf.at[e, c], wf.at[e, c], mate)

    def forward_x(step):
        if step == 0:
            part_x(0, 1, low, (4, 1))
            part_x(2, 2, high, (5, 3))
        if step == 1:
            part_x(1, 1, high)
            part_x(3, 2, low)
            to_mate(0, shard_x(1, zl))
            to_mate(1, shard_x(2, zl))
        if step == 2:
            part_x(4, 3, low)
            part_x(5, 3, high)
            to_mate(2, shard_x(3, zl))

    def forward_z(i):
        e = shard_x(i, 1 - zl)
        rc(WZ + 2 * i, wf.at[e, c, low], wf.at[e, c, low], mate).wait_recv()
        rc(WZ + 2 * i + 1, wf.at[e, c, high], wf.at[e, c, high], mate).wait_recv()
        to_mate(3 + i, e)

    def from_mate(j, e):
        rc(WC + j, wf.at[e, 1 - c], wf.at[e, 1 - c], mate).wait_recv()

    for load in loads[:3]:
        load.wait()

    class Ring:
        def __init__(self, base, v, to, piece, slot):
            self.base, self.v, self.piece, self.slot = base, v, piece, slot
            self.up, self.down = to(1), to(3)

        def start(self):
            v, piece, slot = self.v, self.piece, self.slot
            send(self.base, piece(turn(v, 2), 0), slot(0), self.up)
            send(self.base + 1, piece(turn(v, 2), 1), slot(1), self.down)
            send(self.base + 2, piece(turn(v, 1), 1), slot(2), self.up)
            send(self.base + 3, piece(turn(v, 3), 0), slot(3), self.down)

        def relay(self):
            for part, n, to in ((0, 1, self.up), (1, 3, self.down)):
                mid, got = self.piece(turn(self.v, n), part), self.slot(part)
                rc(self.base + part, got, got, mate).wait_recv()
                mid[...] = (mid[...].astype(F32) + got[...].astype(F32)).astype(BF16)
                send(self.base + 4 + part, mid, self.slot(4 + part), to)

        def wait(self):
            for n in range(2, 6):
                rc(self.base + n, self.slot(n), self.slot(n), mate).wait_recv()

    def ring_of_y(k):
        return Ring(
            Y1 + 6 * k, y, to_y, lambda to, part: g_y.at[to, 2 * k + part], lambda n: r_y1.at[n, k]
        )

    ring_y = [ring_of_y(k) for k in range(HK)]
    ring_x = Ring(X1, x, to_x, lambda to, part: g_x.at[to, part], lambda n: r_x1.at[n])
    ring_z = Ring(Z1, z, to_z, lambda to, part: g_z.at[to, part], lambda n: r_z1.at[n])

    def head(h):
        return pl.ds(pl.multiple_of(h * DH, DH), DH)

    def fwd(k):
        for n in (2 * k, 2 * k + 1):
            rc(*halo(n)).wait_recv()
        keys, values = kv[0, :, head(k)], kv[1, :, head(k)]

        def one(g, _):
            h = k * 4 + g
            scores = dg(q_v[:, head(h)], keys, 1, 1) * SCALE + bias[...]
            e = jnp.exp(scores - jnp.max(scores, axis=-1, keepdims=True))
            p = (e * (1.0 / jnp.sum(e, axis=-1, keepdims=True))).astype(BF16)
            prob[h] = p
            att[:, head(h)] = dg(p, values, 1, 0).astype(BF16)
            return 0

        lax.fori_loop(0, 4, one, 0, unroll=True)
        cols = pl.ds(k * 512, 512)
        send(ATT + k, att.at[:, cols], attm.at[:, cols], mate)

    def grad_w(k):
        cols = pl.ds(k * 512, 512)
        rc(ATT + k, att.at[:, cols], attm.at[:, cols], mate).wait_recv()
        if k == 0:
            loads[3].wait()
            rc(COT, cotm, cotm, mate).wait_recv()
        for e in (2 * k, 2 * k + 1):
            own = att[:, e * 256 : (e + 1) * 256]
            other = attm[:, e * 256 : (e + 1) * 256]
            for n in range(4):
                mine = cot_v[:, pl.ds(pl.multiple_of(c * 1024 + n * 256, 256), 256)]
                part = dg(own, mine, 0, 0) + dg(other, cotm[:, n * 256 : (n + 1) * 256], 0, 0)
                part = part.astype(BF16)
                for sub in range(8):
                    rows = part[sub * 32 : (sub + 1) * 32]
                    if n < 2:
                        g_y[sub % 4, e, sub // 4, :, n * 256 : (n + 1) * 256] = rows
                    elif n == 2:
                        g_x[e % 4, e // 4, sub, :, 0:256] = rows
                    else:
                        g_x[e % 4, e // 4, sub, :, 256:384] = rows[:, 0:128]
                        g_z[sub // 4 * 2 + e // 4, e % 4 // 2, e % 2, sub % 4] = rows[:, 128:256]
    fwd(0)
    fwd(1)
    grad_w(0)
    ring_y[0].start()
    fwd(2)
    forward_x(0)
    grad_w(1)
    ring_y[1].start()
    ring_y[0].relay()
    fwd(3)
    grad_w(2)
    ring_y[2].start()
    ring_y[1].relay()
    forward_x(1)
    grad_w(3)
    ring_y[3].start()
    ring_x.start()
    ring_z.start()
    ring_y[2].relay()
    forward_z(0)
    loads[4].wait()

    def bwd(e):
        k = lax.div(e, 2)
        weight = wf[e].reshape(256, DM)
        grad = dg(cot_v[...], weight, 1, 1).astype(BF16)
        keys, values = kv[0, :, head(k)], kv[1, :, head(k)]
        for g in range(2):
            h = 2 * e + g
            grad_h = grad[:, g * DH : (g + 1) * DH]
            delta = jnp.sum(
                grad_h.astype(F32) * att[:, head(h)].astype(F32), axis=-1, keepdims=True
            )
            p = prob[h]
            grad_s = (p.astype(F32) * (dg(grad_h, values, 1, 1) - delta)).astype(BF16)
            gq_v[:, head(h)] = (dg(grad_s, keys, 1, 0) * SCALE).astype(BF16)
            gk_t[head(k), :] += dg(q_v[:, head(h)], grad_s, 0, 0)
            gv_t[head(k), :] += dg(grad_h, p, 0, 0)

    def bwd_x(i):
        e = shard_x(i, zl)
        from_mate(i - 1, e)
        bwd(e)

    def bwd_z(i):
        e = shard_x(i, 1 - zl)
        from_mate(3 + i, e)
        bwd(e)

    def arrived(base, dst, source):
        for n in range(3):
            rc(base + n, source, dst.at[n], mate).wait_recv()

    def total(own, got, *where):
        out = own.astype(F32)
        for n in range(3):
            out = out + got[(n, *where)].astype(F32)
        return out

    def settled(own, got, part, *where):
        one, two = ((3, 4), (2, 5))[part]
        return own.astype(F32) + got[(one, *where)].astype(F32) + got[(two, *where)].astype(F32)

    def project(n, _):
        cols = pl.ds(n * 256, 256)
        weight = wf[:, :, :, cols].reshape(2048, 256)
        pro_v[:, cols] = dg(att[...], weight, 1, 0).astype(BF16)
        return 0

    def sum_z():
        ring_z.wait()
        for x_ in range(4):
            for y_ in range(4):
                where = (x_ % 2, y_)
                value = settled(g_z[(z, x_ // 2, *where)], r_z1, x_ // 2, *where)
                s_z[x_, y_] = value.astype(BF16)
        for n in (1, 3, 2):
            send(Z2 + n - 1, s_z.at[turn(x, n)], r_z2.at[n - 1], to_x(n))

    def sum_y():
        for ring in ring_y:
            ring.wait()
        for e in range(8):
            for zh_ in range(2):
                value = settled(g_y[y, e, zh_], r_y1, e % 2, e // 2, zh_)
                s_y[zh_ * 2 + e // 4, e % 4] = value.astype(BF16)
        for n in (1, 3, 2):
            send(Y2 + n - 1, s_y.at[turn(z, n)], r_y2.at[n - 1], to_z(n))

    def sum_x():
        ring_x.wait()
        for zl_ in range(2):
            for sub in range(8):
                value = settled(g_x[x, zl_, sub], r_x1, zl_, sub)
                s_x[sub % 4, sub // 4 * 2 + zl_] = value.astype(BF16)
        for n in (1, 3, 2):
            send(X2 + n - 1, s_x.at[turn(y, n)], r_x2.at[n - 1], to_y(n))

    def give_back(part):
        heads = pl.ds(pl.multiple_of((zl if part == 0 else 1 - zl) * 256, 256), 256)
        back_s[0, :, heads] = (gk_t[heads, 0:TOK].T * SCALE).astype(BF16)
        back_s[1, :, heads] = gv_t[heads, 0:TOK].T.astype(BF16)
        for n in range(2):
            send(BACK + 2 * part + n, back_s.at[n, :, heads], back_r.at[n, :, heads], before)

    bwd(d)
    forward_x(2)
    bwd_x(1)
    bwd_x(2)
    ring_y[3].relay()
    forward_z(1)
    bwd_z(0)
    forward_z(2)
    bwd_x(3)
    give_back(0)
    ring_x.relay()
    ring_z.relay()
    bwd_z(1)
    sum_y()
    bwd_z(2)
    forward_z(3)
    sum_z()
    sum_x()
    bwd_z(3)
    give_back(1)

    for n in range(6):
        project(n, 0)
    arrived(Y2, r_y2, s_y.at[0])
    for x_ in range(4):
        s_y2[x_] = total(s_y[z, x_], r_y2, x_).astype(BF16)
    for n in (1, 3, 2):
        send(Y3 + n - 1, s_y2.at[turn(x, n)], r_y3.at[n - 1], to_x(n))
    arrived(Z2, r_z2, s_z.at[0])
    for y_ in range(4):
        s_z2[y_] = total(s_z[x, y_], r_z2, y_).astype(BF16)
    for n in (1, 3, 2):
        send(Z3 + n - 1, s_z2.at[turn(y, n)], r_z3.at[n - 1], to_y(n))
    arrived(X2, r_x2, s_x.at[0])
    for z_ in range(4):
        s_x2[z_] = total(s_x[y, z_], r_x2, z_).astype(BF16)
    for n in (1, 3, 2):
        send(X3 + n - 1, s_x2.at[turn(z, n)], r_x3.at[n - 1], to_z(n))
    for n in range(6, 8):
        project(n, 0)
    outs = [
        pltpu.make_async_copy(pro_v, pro_hbm, osem.at[0]),
        pltpu.make_async_copy(gq_v, gq_hbm, osem.at[1]),
    ]
    for out in outs:
        out.start()


    factor = 1.0 / math.sqrt(TOTAL)
    piece_of = zh * 4 + y

    def gather(chunk):
        piece = agb.at[chunk, c, piece_of]
        for n in range(7):
            send(AG + 7 * chunk + n, piece, piece, to_y(n + 1) if n < 3 else to_o(n - 3))

    def origin(n):
        return zh * 4 + turn(y, 3 - n) if n < 3 else (1 - zh) * 4 + turn(y, 7 - n)

    def gathered(chunk, part):
        for n in (range(3), range(3, 7))[part]:
            piece = agb.at[chunk, c, origin(n)]
            rc(AG + 7 * chunk + n, piece, piece, mate).wait_recv()
        which = zh if part == 0 else 1 - zh
        half = agb.at[chunk, c, pl.ds(which * 4, 4)]
        send(AGC + 2 * chunk + part, half, half, mate)

    def finished(chunk):
        for part, which in enumerate((zh, 1 - zh)):
            half = agb.at[chunk, 1 - c, pl.ds(which * 4, 4)]
            rc(AGC + 2 * chunk + part, half, half, mate).wait_recv()
        outs.append(pltpu.make_async_copy(agb.at[chunk], gw_hbm.at[chunk], osem.at[4 + chunk]))
        outs[-1].start()

    arrived(Y3, r_y3, s_y2.at[0])
    agb[0, c, piece_of] = (total(s_y2[x], r_y3) * factor).astype(BF16)
    gather(0)
    arrived(Z3, r_z3, s_z2.at[0])
    agb[1, c, piece_of, :, 384:512] = (total(s_z2[y], r_z3) * factor).astype(BF16)
    arrived(X3, r_x3, s_x2.at[0])
    agb[1, c, piece_of, :, 0:384] = (total(s_x2[z], r_x3) * factor).astype(BF16)
    gather(1)

    for part in range(2):
        heads = pl.ds(pl.multiple_of((zl if part == 0 else 1 - zl) * 256, 256), 256)
        for n in range(2):
            got = back_r.at[n, :, heads]
            rc(BACK + 2 * part + n, got, got, before).wait_recv()
    gkv_v[0] = (gk_t[:, TOK : 2 * TOK].T * SCALE + back_r[0].astype(F32)).astype(BF16)
    gkv_v[1] = (gv_t[:, TOK : 2 * TOK].T + back_r[1].astype(F32)).astype(BF16)
    for n, out in enumerate((gk_hbm, gv_hbm)):
        outs.append(pltpu.make_async_copy(gkv_v.at[n], out, osem.at[2 + n]))
        outs[-1].start()

    gathered(0, 0)
    gathered(1, 0)
    gathered(0, 1)
    finished(0)
    gathered(1, 1)
    finished(1)
    for copy in sent:
        copy.wait_send()
    for out in outs:
        out.wait()


def finish(
    pro, gq, gk, gv, gw, pro_o, gq_o, gk_o, gv_o, gw_o,
    pro_v, gq_v, gk_v, gv_v, gw_v, wide, in_sem, out_sem,
):
    pieces = [(gw.at[a, b], gw_v.at[a, b], (a, b)) for a in range(2) for b in range(2)]
    for source, held, out in ((pro, pro_v, pro_o), (gq, gq_v, gq_o)):
        for n in range(2):
            rows = pl.ds(n * 128, 128)
            pieces.append((source.at[rows], held.at[rows], out.at[rows]))
    pieces += [(gk, gk_v, gk_o), (gv, gv_v, gv_o)]
    got = [
        pltpu.make_async_copy(source, held, in_sem.at[n])
        for n, (source, held, _) in enumerate(pieces)
    ]
    for copy in got:
        copy.start()
    put = []
    for n, (_, held, out) in enumerate(pieces):
        got[n].wait()
        if n < 4:
            a, b = out
            cols = pl.ds(b * 1024 + a * 512, 512)
            wide[:, cols] = gw_v[a, b].reshape(TOK, 512).astype(F32)
            held, out = wide.at[:, cols], gw_o.at[:, cols]
        put.append(pltpu.make_async_copy(held, out, out_sem.at[n]))
        put[n].start()
    for copy in put:
        copy.wait()


def body(queries, key_heads, value_heads, doc_lengths, out_weight, cotangent):
    anywhere = pl.BlockSpec(memory_space=pl.ANY)
    shapes = [
        ((TOK, 2048), BF16),
        ((TOK, 2048), BF16),
        ((2, 512, 512), BF16),
        ((8, 2, 128, 2048), BF16),
        ((TOK, 1024), BF16),
        ((TOK, 2048), BF16),
        ((TOK, 2048), BF16),
        ((HQ, TOK, 512), BF16),
        ((TOK, 512), F32),
        ((4, 8, 2, 32, 512), BF16),
        ((6, 4, 2, 32, 512), BF16),
        ((4, 4, 32, 512), BF16),
        ((3, 4, 32, 512), BF16),
        ((4, 32, 512), BF16),
        ((3, 32, 512), BF16),
        ((4, 2, 8, 32, 384), BF16),
        ((6, 8, 32, 384), BF16),
        ((4, 4, 32, 384), BF16),
        ((3, 4, 32, 384), BF16),
        ((4, 32, 384), BF16),
        ((3, 32, 384), BF16),
        ((4, 2, 2, 4, 32, 128), BF16),
        ((6, 2, 4, 32, 128), BF16),
        ((4, 4, 32, 128), BF16),
        ((3, 4, 32, 128), BF16),
        ((4, 32, 128), BF16),
        ((3, 32, 128), BF16),
        ((2, 2, 8, 32, 512), BF16),
        ((512, 512), F32),
        ((512, 512), F32),
        ((2, TOK, 512), BF16),
        ((2, TOK, 512), BF16),
        ((TOK, 2048), BF16),
        ((TOK, 2048), BF16),
        ((2, TOK, 512), BF16),
    ]
    scratch = [pltpu.VMEM(shape, dtype) for shape, dtype in shapes]
    scratch += [pltpu.SemaphoreType.DMA((n,)) for n in (COPIES, COPIES, 5, 6)]
    results = [
        jax.ShapeDtypeStruct((TOK, 2048), BF16),
        jax.ShapeDtypeStruct((TOK, 2048), BF16),
        jax.ShapeDtypeStruct((TOK, 512), BF16),
        jax.ShapeDtypeStruct((TOK, 512), BF16),
    ]
    outs = pl.pallas_call(
        kernel,
        out_shape=[*results, jax.ShapeDtypeStruct((2, 2, 8, 32, 512), BF16)],
        in_specs=[pl.BlockSpec(memory_space=pltpu.SMEM)] + [anywhere] * 5,
        out_specs=[anywhere] * 5,
        scratch_shapes=scratch,
        compiler_params=pltpu.CompilerParams(
            collective_id=0, has_side_effects=True, vmem_limit_bytes=56 << 20
        ),
        cost_estimate=pl.CostEstimate(
            flops=10_000_000_000, bytes_accessed=12_000_000, transcendentals=2_000_000
        ),
    )(
        doc_lengths,
        queries[0],
        key_heads[0],
        value_heads[0],
        out_weight.reshape(2, 128, DM),
        cotangent[0],
    )
    outs = pl.pallas_call(
        finish,
        out_shape=[*results, jax.ShapeDtypeStruct((TOK, 2048), F32)],
        in_specs=[anywhere] * 5,
        out_specs=[anywhere] * 5,
        scratch_shapes=[
            *(pltpu.VMEM(result.shape, BF16) for result in results),
            pltpu.VMEM((2, 2, 8, 32, 512), BF16),
            pltpu.VMEM((TOK, 2048), F32),
            pltpu.SemaphoreType.DMA((10,)),
            pltpu.SemaphoreType.DMA((10,)),
        ],
    )(*outs)
    return (*(out[None] for out in outs[:4]), outs[4])


def solution(mesh):
    tokens = P("dp", "seq", None)
    rows = P("dp", None)
    return jax.shard_map(
        body,
        mesh=mesh,
        in_specs=(tokens, tokens, tokens, rows, rows, tokens),
        out_specs=(tokens, tokens, tokens, tokens, rows),
        check_vma=False,
    )
```

```python
import math

import jax
import jax.numpy as jnp
from jax import lax
from jax.experimental import pallas as pl
from jax.experimental.pallas import tpu as pltpu
from jax.sharding import PartitionSpec as P

HQ = 16
HK = 4
DH = 128
DM = 2048
TOK = 256
DOCS = 32
TOTAL = 32768
SCALE = 1.0 / math.sqrt(DH)
LOG2E = math.log2(math.e)
F32 = jnp.float32
BF16 = jnp.bfloat16
MESH = pl.DeviceIdType.MESH

HALO = 0
WX = HALO + 8
WZ = WX + 6
WC = WZ + 8
COT = WC + 7
ATT = COT + 1
Y1 = ATT + 4
X1 = Y1 + 24
Z1 = X1 + 6
Y2 = Z1 + 6
X2 = Y2 + 3
Z2 = X2 + 3
Y3 = Z2 + 3
X3 = Y3 + 3
Z3 = X3 + 3
BACK = Z3 + 3
AG = BACK + 4
AGC = AG + 14
COPIES = AGC + 4


def dg(a, b, ca, cb):
    return lax.dot_general(a, b, (((ca,), (cb,)), ((), ())), preferred_element_type=F32)


def kernel(
    len_ref, q_hbm, k_hbm, v_hbm, w_hbm, cot_hbm,
    pro_hbm, gq_hbm, gk_hbm, gv_hbm, gw_hbm,
    q_v, cot_v, kv, wf, cotm, att, attm, prob, bias, inverse,
    g_y, r_y1, s_y, r_y2, s_y2, r_y3,
    g_x, r_x1, s_x, r_x2, s_x2, r_x3,
    g_z, r_z1, s_z, r_z2, s_z2, r_z3,
    agb, gk_t, gv_t, back_s, back_r,
    pro_v, gq_v, gkv_v,
    ssem, rsem, lsem, osem,
):
    s = lax.axis_index("seq")
    d = lax.axis_index("dp")
    zh = lax.div(s, 8)
    y = lax.rem(lax.div(s, 2), 4)
    c = lax.rem(s, 2)
    zl = lax.div(d, 4)
    x = lax.rem(d, 4)
    z = zh * 2 + zl

    def at(zh_, y_, c_, zl_, x_):
        return {"seq": zh_ * 8 + y_ * 2 + c_, "dp": zl_ * 4 + x_}

    def turn(v, n):
        return lax.rem(v + n, 4)

    def to_x(n):
        return at(zh, y, c, zl, turn(x, n))

    def to_y(n):
        return at(zh, turn(y, n), c, zl, x)

    def to_z(n):
        zz = turn(z, n)
        return at(lax.div(zz, 2), y, c, lax.rem(zz, 2), x)

    def to_o(n):
        return at(1 - zh, turn(y, n), c, zl, x)

    mate = at(zh, y, 1 - c, zl, x)
    near = at(zh, y, c, 1 - zl, x)
    far = at(1 - zh, y, c, 1 - zl, x)
    after = {"seq": lax.rem(s + 1, 16), "dp": d}
    before = {"seq": lax.rem(s + 15, 16), "dp": d}

    def rc(n, src, dst, to):
        return pltpu.make_async_remote_copy(
            src_ref=src, dst_ref=dst, send_sem=ssem.at[n], recv_sem=rsem.at[n],
            device_id=to, device_id_type=MESH,
        )

    sent = []

    def send(n, src, dst, to):
        copy = rc(n, src, dst, to)
        copy.start()
        sent.append(copy)

    loads = [
        pltpu.make_async_copy(k_hbm, kv.at[0, pl.ds(TOK, TOK)], lsem.at[0]),
        pltpu.make_async_copy(v_hbm, kv.at[1, pl.ds(TOK, TOK)], lsem.at[1]),
        pltpu.make_async_copy(q_hbm, q_v, lsem.at[2]),
        pltpu.make_async_copy(cot_hbm, cot_v, lsem.at[3]),
        pltpu.make_async_copy(w_hbm, wf.at[d], lsem.at[4]),
    ]
    for load in loads:
        load.start()

    barrier = pltpu.get_barrier_semaphore()
    peers = [mate, after, before]
    peers += [f(n) for f in (to_x, to_y, to_z) for n in (1, 2, 3)]
    peers += [to_o(n) for n in (1, 2, 3)]
    for peer in peers:
        pl.semaphore_signal(barrier, inc=1, device_id=peer, device_id_type=MESH)

    first = s * TOK
    q_pos = first + lax.broadcasted_iota(jnp.int32, (TOK, 1), 0)
    begin = jnp.zeros((TOK, 1), jnp.int32)
    opening = len_ref[0, 0] * 0
    for n in range(DOCS):
        begin = jnp.where(q_pos >= opening, opening, begin)
        opening = opening + len_ref[0, n]
    k_pos = first - TOK + lax.broadcasted_iota(jnp.int32, (TOK, 2 * TOK), 1)
    bias[...] = jnp.where((k_pos >= begin) & (k_pos <= q_pos), 0.0, -1e30)
    gk_t[...] = jnp.zeros_like(gk_t)
    gv_t[...] = jnp.zeros_like(gv_t)

    pl.semaphore_wait(barrier, len(peers))

    prev = pl.ds(0, TOK)
    low, high = pl.ds(0, 64), pl.ds(64, 64)

    def halo(n):
        cols = pl.ds(n // 2 * DH, DH)
        source = (k_hbm, v_hbm)[n % 2]
        return HALO + n, source.at[:, cols], kv.at[n % 2, prev, cols], after

    for n in range(8):
        send(*halo(n))
    send(WX, w_hbm.at[c, low], wf.at[d, c, low], to_x(1))
    send(WX + 2, w_hbm.at[c, high], wf.at[d, c, high], to_x(3))
    send(WX + 1, w_hbm.at[c, high], wf.at[d, c, high], to_x(1))
    send(WX + 3, w_hbm.at[c, low], wf.at[d, c, low], to_x(3))
    send(WZ, w_hbm.at[c, low], wf.at[d, c, low], near)
    send(WZ + 1, w_hbm.at[c, high], wf.at[d, c, high], far)
    send(COT, cot_hbm.at[:, pl.ds(pl.multiple_of((1 - c) * 1024, 1024), 1024)], cotm, mate)

    def shard_x(i, plane):
        return plane * 4 + turn(x, (0, 3, 1, 2)[i])

    def part_x(n, i, part, relay=None):
        piece = wf.at[shard_x(i, zl), c, part]
        rc(WX + n, piece, piece, mate).wait_recv()
        if relay is not None:
            send(WX + relay[0], piece, piece, to_x(relay[1]))
        if part is low:
            send(WZ + 2 * i, piece, piece, near)
        else:
            send(WZ + 2 * i + 1, piece, piece, far)

    def to_mate(j, e):
        send(WC + j, wf.at[e, c], wf.at[e, c], mate)

    def forward_x(step):
        if step == 0:
            part_x(0, 1, low, (4, 1))
            part_x(2, 2, high, (5, 3))
        if step == 1:
            part_x(1, 1, high)
            part_x(3, 2, low)
            to_mate(0, shard_x(1, zl))
            to_mate(1, shard_x(2, zl))
        if step == 2:
            part_x(4, 3, low)
            part_x(5, 3, high)
            to_mate(2, shard_x(3, zl))

    def forward_z(i):
        e = shard_x(i, 1 - zl)
        rc(WZ + 2 * i, wf.at[e, c, low], wf.at[e, c, low], mate).wait_recv()
        rc(WZ + 2 * i + 1, wf.at[e, c, high], wf.at[e, c, high], mate).wait_recv()
        to_mate(3 + i, e)

    def from_mate(j, e):
        rc(WC + j, wf.at[e, 1 - c], wf.at[e, 1 - c], mate).wait_recv()

    for load in loads[:3]:
        load.wait()

    class Ring:
        def __init__(self, base, v, to, piece, slot):
            self.base, self.v, self.piece, self.slot = base, v, piece, slot
            self.up, self.down = to(1), to(3)

        def start(self):
            v, piece, slot = self.v, self.piece, self.slot
            send(self.base, piece(turn(v, 2), 0), slot(0), self.up)
            send(self.base + 1, piece(turn(v, 2), 1), slot(1), self.down)
            send(self.base + 2, piece(turn(v, 1), 1), slot(2), self.up)
            send(self.base + 3, piece(turn(v, 3), 0), slot(3), self.down)

        def relay(self):
            for part, n, to in ((0, 1, self.up), (1, 3, self.down)):
                mid, got = self.piece(turn(self.v, n), part), self.slot(part)
                rc(self.base + part, got, got, mate).wait_recv()
                mid[...] = (mid[...].astype(F32) + got[...].astype(F32)).astype(BF16)
                send(self.base + 4 + part, mid, self.slot(4 + part), to)

        def wait(self):
            for n in range(2, 6):
                rc(self.base + n, self.slot(n), self.slot(n), mate).wait_recv()

    def ring_of_y(k):
        return Ring(
            Y1 + 6 * k, y, to_y, lambda to, part: g_y.at[to, 2 * k + part], lambda n: r_y1.at[n, k]
        )

    ring_y = [ring_of_y(k) for k in range(HK)]
    ring_x = Ring(X1, x, to_x, lambda to, part: g_x.at[to, part], lambda n: r_x1.at[n])
    ring_z = Ring(Z1, z, to_z, lambda to, part: g_z.at[to, part], lambda n: r_z1.at[n])

    def head(h):
        return pl.ds(pl.multiple_of(h * DH, DH), DH)

    def fwd(k):
        for n in (2 * k, 2 * k + 1):
            rc(*halo(n)).wait_recv()
        keys, values = kv[0, :, head(k)], kv[1, :, head(k)]

        wide = jnp.concatenate([values, jnp.ones_like(values)], axis=1)

        def one(g, _):
            h = k * 4 + g
            scores = dg(q_v[:, head(h)], keys, 1, 1) * (SCALE * LOG2E) + bias[...]
            e = jnp.exp2(scores - jnp.max(scores, axis=-1, keepdims=True)).astype(BF16)
            prob[h] = e
            out = dg(e, wide, 1, 0)
            inv = 1.0 / out[:, DH:]
            inverse[:, head(h)] = inv
            att[:, head(h)] = (out[:, :DH] * inv).astype(BF16)
            return 0

        lax.fori_loop(0, 4, one, 0, unroll=True)
        cols = pl.ds(k * 512, 512)
        send(ATT + k, att.at[:, cols], attm.at[:, cols], mate)

    def grad_w(k):
        cols = pl.ds(k * 512, 512)
        rc(ATT + k, att.at[:, cols], attm.at[:, cols], mate).wait_recv()
        if k == 0:
            loads[3].wait()
            rc(COT, cotm, cotm, mate).wait_recv()
        for e in (2 * k, 2 * k + 1):
            own = att[:, e * 256 : (e + 1) * 256]
            other = attm[:, e * 256 : (e + 1) * 256]
            for n in range(4):
                mine = cot_v[:, pl.ds(pl.multiple_of(c * 1024 + n * 256, 256), 256)]
                part = dg(own, mine, 0, 0) + dg(other, cotm[:, n * 256 : (n + 1) * 256], 0, 0)
                part = part.astype(BF16)
                for sub in range(8):
                    rows = part[sub * 32 : (sub + 1) * 32]
                    if n < 2:
                        g_y[sub % 4, e, sub // 4, :, n * 256 : (n + 1) * 256] = rows
                    elif n == 2:
                        g_x[e % 4, e // 4, sub, :, 0:256] = rows
                    else:
                        g_x[e % 4, e // 4, sub, :, 256:384] = rows[:, 0:128]
                        g_z[sub // 4 * 2 + e // 4, e % 4 // 2, e % 2, sub % 4] = rows[:, 128:256]
    fwd(0)
    fwd(1)
    grad_w(0)
    ring_y[0].start()
    forward_x(0)
    fwd(2)
    grad_w(1)
    ring_y[1].start()
    ring_y[0].relay()
    fwd(3)
    grad_w(2)
    ring_y[2].start()
    ring_y[1].relay()
    forward_x(1)
    grad_w(3)
    ring_y[3].start()
    ring_x.start()
    ring_z.start()
    ring_y[2].relay()
    forward_z(0)
    loads[4].wait()

    def bwd(e):
        k = lax.div(e, 2)
        weight = wf[e].reshape(256, DM)
        grad = dg(cot_v[...], weight, 1, 1).astype(BF16)
        keys, values = kv[0, :, head(k)], kv[1, :, head(k)]
        for g in range(2):
            h = 2 * e + g
            grad_h = grad[:, g * DH : (g + 1) * DH]
            delta = jnp.sum(
                grad_h.astype(F32) * att[:, head(h)].astype(F32), axis=-1, keepdims=True
            )
            p = prob[h]
            inv = inverse[:, head(h)]
            grad_n = (grad_h.astype(F32) * inv).astype(BF16)
            inv = jnp.concatenate([inv] * 4, axis=1)
            grad_s = (p.astype(F32) * ((dg(grad_h, values, 1, 1) - delta) * inv)).astype(BF16)
            gq_v[:, head(h)] = (dg(grad_s, keys, 1, 0) * SCALE).astype(BF16)
            gk_t[head(k), :] += dg(q_v[:, head(h)], grad_s, 0, 0)
            gv_t[head(k), :] += dg(grad_n, p, 0, 0)

    def bwd_x(i):
        e = shard_x(i, zl)
        from_mate(i - 1, e)
        bwd(e)

    def bwd_z(i):
        e = shard_x(i, 1 - zl)
        from_mate(3 + i, e)
        bwd(e)

    def arrived(base, dst, source):
        for n in range(3):
            rc(base + n, source, dst.at[n], mate).wait_recv()

    def total(own, got, *where):
        out = own.astype(F32)
        for n in range(3):
            out = out + got[(n, *where)].astype(F32)
        return out

    def settled(own, got, part, *where):
        one, two = ((3, 4), (2, 5))[part]
        return own.astype(F32) + got[(one, *where)].astype(F32) + got[(two, *where)].astype(F32)

    def project(n, _):
        cols = pl.ds(n * 256, 256)
        weight = wf[:, :, :, cols].reshape(2048, 256)
        pro_v[:, cols] = dg(att[...], weight, 1, 0).astype(BF16)
        return 0

    def sum_z():
        ring_z.wait()
        for x_ in range(4):
            for y_ in range(4):
                where = (x_ % 2, y_)
                value = settled(g_z[(z, x_ // 2, *where)], r_z1, x_ // 2, *where)
                s_z[x_, y_] = value.astype(BF16)
        for n in (1, 3, 2):
            send(Z2 + n - 1, s_z.at[turn(x, n)], r_z2.at[n - 1], to_x(n))

    def sum_y():
        for ring in ring_y:
            ring.wait()
        for e in range(8):
            for zh_ in range(2):
                value = settled(g_y[y, e, zh_], r_y1, e % 2, e // 2, zh_)
                s_y[zh_ * 2 + e // 4, e % 4] = value.astype(BF16)
        for n in (1, 3, 2):
            send(Y2 + n - 1, s_y.at[turn(z, n)], r_y2.at[n - 1], to_z(n))

    def sum_x():
        ring_x.wait()
        for zl_ in range(2):
            for sub in range(8):
                value = settled(g_x[x, zl_, sub], r_x1, zl_, sub)
                s_x[sub % 4, sub // 4 * 2 + zl_] = value.astype(BF16)
        for n in (1, 3, 2):
            send(X2 + n - 1, s_x.at[turn(y, n)], r_x2.at[n - 1], to_y(n))

    def give_back(part):
        heads = pl.ds(pl.multiple_of((zl if part == 0 else 1 - zl) * 256, 256), 256)
        back_s[0, :, heads] = (gk_t[heads, 0:TOK].T * SCALE).astype(BF16)
        back_s[1, :, heads] = gv_t[heads, 0:TOK].T.astype(BF16)
        for n in range(2):
            send(BACK + 2 * part + n, back_s.at[n, :, heads], back_r.at[n, :, heads], before)

    bwd(d)
    forward_x(2)
    bwd_x(1)
    bwd_x(2)
    ring_y[3].relay()
    forward_z(1)
    bwd_z(0)
    forward_z(2)
    bwd_x(3)
    give_back(0)
    ring_x.relay()
    ring_z.relay()
    bwd_z(1)
    sum_y()
    bwd_z(2)
    forward_z(3)
    sum_z()
    sum_x()
    bwd_z(3)
    give_back(1)

    for n in range(6):
        project(n, 0)
    arrived(Y2, r_y2, s_y.at[0])
    for x_ in range(4):
        s_y2[x_] = total(s_y[z, x_], r_y2, x_).astype(BF16)
    for n in (1, 3, 2):
        send(Y3 + n - 1, s_y2.at[turn(x, n)], r_y3.at[n - 1], to_x(n))
    arrived(Z2, r_z2, s_z.at[0])
    for y_ in range(4):
        s_z2[y_] = total(s_z[x, y_], r_z2, y_).astype(BF16)
    for n in (1, 3, 2):
        send(Z3 + n - 1, s_z2.at[turn(y, n)], r_z3.at[n - 1], to_y(n))
    arrived(X2, r_x2, s_x.at[0])
    for z_ in range(4):
        s_x2[z_] = total(s_x[y, z_], r_x2, z_).astype(BF16)
    for n in (1, 3, 2):
        send(X3 + n - 1, s_x2.at[turn(z, n)], r_x3.at[n - 1], to_z(n))
    for n in range(6, 8):
        project(n, 0)
    outs = [
        pltpu.make_async_copy(pro_v, pro_hbm, osem.at[0]),
        pltpu.make_async_copy(gq_v, gq_hbm, osem.at[1]),
    ]
    for out in outs:
        out.start()


    factor = 1.0 / math.sqrt(TOTAL)
    piece_of = zh * 4 + y

    def gather(chunk):
        piece = agb.at[chunk, c, piece_of]
        for n in range(7):
            send(AG + 7 * chunk + n, piece, piece, to_y(n + 1) if n < 3 else to_o(n - 3))

    def origin(n):
        return zh * 4 + turn(y, 3 - n) if n < 3 else (1 - zh) * 4 + turn(y, 7 - n)

    def gathered(chunk, part):
        for n in (range(3), range(3, 7))[part]:
            piece = agb.at[chunk, c, origin(n)]
            rc(AG + 7 * chunk + n, piece, piece, mate).wait_recv()
        which = zh if part == 0 else 1 - zh
        half = agb.at[chunk, c, pl.ds(which * 4, 4)]
        send(AGC + 2 * chunk + part, half, half, mate)

    def finished(chunk):
        for part, which in enumerate((zh, 1 - zh)):
            half = agb.at[chunk, 1 - c, pl.ds(which * 4, 4)]
            rc(AGC + 2 * chunk + part, half, half, mate).wait_recv()
        outs.append(pltpu.make_async_copy(agb.at[chunk], gw_hbm.at[chunk], osem.at[4 + chunk]))
        outs[-1].start()

    arrived(Y3, r_y3, s_y2.at[0])
    agb[0, c, piece_of] = (total(s_y2[x], r_y3) * factor).astype(BF16)
    gather(0)
    arrived(Z3, r_z3, s_z2.at[0])
    agb[1, c, piece_of, :, 384:512] = (total(s_z2[y], r_z3) * factor).astype(BF16)
    arrived(X3, r_x3, s_x2.at[0])
    agb[1, c, piece_of, :, 0:384] = (total(s_x2[z], r_x3) * factor).astype(BF16)
    gather(1)

    for part in range(2):
        heads = pl.ds(pl.multiple_of((zl if part == 0 else 1 - zl) * 256, 256), 256)
        for n in range(2):
            got = back_r.at[n, :, heads]
            rc(BACK + 2 * part + n, got, got, before).wait_recv()
    gkv_v[0] = (gk_t[:, TOK : 2 * TOK].T * SCALE + back_r[0].astype(F32)).astype(BF16)
    gkv_v[1] = (gv_t[:, TOK : 2 * TOK].T + back_r[1].astype(F32)).astype(BF16)
    for n, out in enumerate((gk_hbm, gv_hbm)):
        outs.append(pltpu.make_async_copy(gkv_v.at[n], out, osem.at[2 + n]))
        outs[-1].start()

    gathered(0, 0)
    gathered(1, 0)
    gathered(0, 1)
    finished(0)
    gathered(1, 1)
    finished(1)
    for copy in sent:
        copy.wait_send()
    for out in outs:
        out.wait()


def finish(
    pro, gq, gk, gv, gw, pro_o, gq_o, gk_o, gv_o, gw_o,
    pro_v, gq_v, gk_v, gv_v, gw_v, wide, in_sem, out_sem,
):
    pieces = [(gw.at[a, b], gw_v.at[a, b], (a, b)) for a in range(2) for b in range(2)]
    for source, held, out in ((pro, pro_v, pro_o), (gq, gq_v, gq_o)):
        for n in range(2):
            rows = pl.ds(n * 128, 128)
            pieces.append((source.at[rows], held.at[rows], out.at[rows]))
    pieces += [(gk, gk_v, gk_o), (gv, gv_v, gv_o)]
    got = [
        pltpu.make_async_copy(source, held, in_sem.at[n])
        for n, (source, held, _) in enumerate(pieces)
    ]
    for copy in got:
        copy.start()
    put = []
    for n, (_, held, out) in enumerate(pieces):
        got[n].wait()
        if n < 4:
            a, b = out
            cols = pl.ds(b * 1024 + a * 512, 512)
            wide[:, cols] = gw_v[a, b].reshape(TOK, 512).astype(F32)
            held, out = wide.at[:, cols], gw_o.at[:, cols]
        put.append(pltpu.make_async_copy(held, out, out_sem.at[n]))
        put[n].start()
    for copy in put:
        copy.wait()


def body(queries, key_heads, value_heads, doc_lengths, out_weight, cotangent):
    anywhere = pl.BlockSpec(memory_space=pl.ANY)
    shapes = [
        ((TOK, 2048), BF16),
        ((TOK, 2048), BF16),
        ((2, 512, 512), BF16),
        ((8, 2, 128, 2048), BF16),
        ((TOK, 1024), BF16),
        ((TOK, 2048), BF16),
        ((TOK, 2048), BF16),
        ((HQ, TOK, 512), BF16),
        ((TOK, 512), F32),
        ((TOK, 2048), F32),
        ((4, 8, 2, 32, 512), BF16),
        ((6, 4, 2, 32, 512), BF16),
        ((4, 4, 32, 512), BF16),
        ((3, 4, 32, 512), BF16),
        ((4, 32, 512), BF16),
        ((3, 32, 512), BF16),
        ((4, 2, 8, 32, 384), BF16),
        ((6, 8, 32, 384), BF16),
        ((4, 4, 32, 384), BF16),
        ((3, 4, 32, 384), BF16),
        ((4, 32, 384), BF16),
        ((3, 32, 384), BF16),
        ((4, 2, 2, 4, 32, 128), BF16),
        ((6, 2, 4, 32, 128), BF16),
        ((4, 4, 32, 128), BF16),
        ((3, 4, 32, 128), BF16),
        ((4, 32, 128), BF16),
        ((3, 32, 128), BF16),
        ((2, 2, 8, 32, 512), BF16),
        ((512, 512), F32),
        ((512, 512), F32),
        ((2, TOK, 512), BF16),
        ((2, TOK, 512), BF16),
        ((TOK, 2048), BF16),
        ((TOK, 2048), BF16),
        ((2, TOK, 512), BF16),
    ]
    scratch = [pltpu.VMEM(shape, dtype) for shape, dtype in shapes]
    scratch += [pltpu.SemaphoreType.DMA((n,)) for n in (COPIES, COPIES, 5, 6)]
    results = [
        jax.ShapeDtypeStruct((TOK, 2048), BF16),
        jax.ShapeDtypeStruct((TOK, 2048), BF16),
        jax.ShapeDtypeStruct((TOK, 512), BF16),
        jax.ShapeDtypeStruct((TOK, 512), BF16),
    ]
    outs = pl.pallas_call(
        kernel,
        out_shape=[*results, jax.ShapeDtypeStruct((2, 2, 8, 32, 512), BF16)],
        in_specs=[pl.BlockSpec(memory_space=pltpu.SMEM)] + [anywhere] * 5,
        out_specs=[anywhere] * 5,
        scratch_shapes=scratch,
        compiler_params=pltpu.CompilerParams(
            collective_id=0, has_side_effects=True, vmem_limit_bytes=56 << 20
        ),
        cost_estimate=pl.CostEstimate(
            flops=10_000_000_000, bytes_accessed=12_000_000, transcendentals=2_000_000
        ),
    )(
        doc_lengths,
        queries[0],
        key_heads[0],
        value_heads[0],
        out_weight.reshape(2, 128, DM),
        cotangent[0],
    )
    outs = pl.pallas_call(
        finish,
        out_shape=[*results, jax.ShapeDtypeStruct((TOK, 2048), F32)],
        in_specs=[anywhere] * 5,
        out_specs=[anywhere] * 5,
        scratch_shapes=[
            *(pltpu.VMEM(result.shape, BF16) for result in results),
            pltpu.VMEM((2, 2, 8, 32, 512), BF16),
            pltpu.VMEM((TOK, 2048), F32),
            pltpu.SemaphoreType.DMA((10,)),
            pltpu.SemaphoreType.DMA((10,)),
        ],
    )(*outs)
    return (*(out[None] for out in outs[:4]), outs[4])


def solution(mesh):
    tokens = P("dp", "seq", None)
    rows = P("dp", None)
    return jax.shard_map(
        body,
        mesh=mesh,
        in_specs=(tokens, tokens, tokens, rows, rows, tokens),
        out_specs=(tokens, tokens, tokens, tokens, rows),
        check_vma=False,
    )
```

```python
import math

import jax
import jax.numpy as jnp
from jax import lax
from jax.experimental import pallas as pl
from jax.experimental.pallas import tpu as pltpu
from jax.sharding import PartitionSpec as P

HQ = 16
HK = 4
DH = 128
DM = 2048
TOK = 256
DOCS = 32
TOTAL = 32768
SCALE = 1.0 / math.sqrt(DH)
LOG2E = math.log2(math.e)
F32 = jnp.float32
BF16 = jnp.bfloat16
MESH = pl.DeviceIdType.MESH

HALO = 0
WX = HALO + 8
WZ = WX + 6
WC = WZ + 8
COT = WC + 7
ATT = COT + 1
Y1 = ATT + 4
X1 = Y1 + 24
Z1 = X1 + 6
Y2 = Z1 + 6
X2 = Y2 + 3
Z2 = X2 + 3
Y3 = Z2 + 3
X3 = Y3 + 3
Z3 = X3 + 3
BACK = Z3 + 3
AG = BACK + 4
AGC = AG + 14
COPIES = AGC + 4


def dg(a, b, ca, cb):
    return lax.dot_general(a, b, (((ca,), (cb,)), ((), ())), preferred_element_type=F32)


def kernel(
    len_ref, q_hbm, k_hbm, v_hbm, w_hbm, cot_hbm,
    pro_hbm, gq_hbm, gk_hbm, gv_hbm, gw_hbm,
    q_v, cot_v, kv, wf, cotm, att, attm, prob, bias, inverse,
    g_y, r_y1, s_y, r_y2, s_y2, r_y3,
    g_x, r_x1, s_x, r_x2, s_x2, r_x3,
    g_z, r_z1, s_z, r_z2, s_z2, r_z3,
    agb, gk_t, gv_t, back_s, back_r,
    pro_v, gq_v, gkv_v,
    ssem, rsem, lsem, osem,
):
    s = lax.axis_index("seq")
    d = lax.axis_index("dp")
    zh = lax.div(s, 8)
    y = lax.rem(lax.div(s, 2), 4)
    c = lax.rem(s, 2)
    zl = lax.div(d, 4)
    x = lax.rem(d, 4)
    z = zh * 2 + zl

    def at(zh_, y_, c_, zl_, x_):
        return {"seq": zh_ * 8 + y_ * 2 + c_, "dp": zl_ * 4 + x_}

    def turn(v, n):
        return lax.rem(v + n, 4)

    def to_x(n):
        return at(zh, y, c, zl, turn(x, n))

    def to_y(n):
        return at(zh, turn(y, n), c, zl, x)

    def to_z(n):
        zz = turn(z, n)
        return at(lax.div(zz, 2), y, c, lax.rem(zz, 2), x)

    def to_o(n):
        return at(1 - zh, turn(y, n), c, zl, x)

    mate = at(zh, y, 1 - c, zl, x)
    near = at(zh, y, c, 1 - zl, x)
    far = at(1 - zh, y, c, 1 - zl, x)
    after = {"seq": lax.rem(s + 1, 16), "dp": d}
    before = {"seq": lax.rem(s + 15, 16), "dp": d}

    def rc(n, src, dst, to):
        return pltpu.make_async_remote_copy(
            src_ref=src, dst_ref=dst, send_sem=ssem.at[n], recv_sem=rsem.at[n],
            device_id=to, device_id_type=MESH,
        )

    sent = []

    def send(n, src, dst, to):
        copy = rc(n, src, dst, to)
        copy.start()
        sent.append(copy)

    loads = [
        pltpu.make_async_copy(k_hbm, kv.at[0, pl.ds(TOK, TOK)], lsem.at[0]),
        pltpu.make_async_copy(v_hbm, kv.at[1, pl.ds(TOK, TOK)], lsem.at[1]),
        pltpu.make_async_copy(q_hbm, q_v, lsem.at[2]),
        pltpu.make_async_copy(cot_hbm, cot_v, lsem.at[3]),
        pltpu.make_async_copy(w_hbm, wf.at[d], lsem.at[4]),
    ]
    for load in loads:
        load.start()

    barrier = pltpu.get_barrier_semaphore()
    peers = [mate, after, before]
    peers += [f(n) for f in (to_x, to_y, to_z) for n in (1, 2, 3)]
    for peer in peers:
        pl.semaphore_signal(barrier, inc=1, device_id=peer, device_id_type=MESH)

    first = s * TOK
    q_pos = first + lax.broadcasted_iota(jnp.int32, (TOK, 1), 0)
    begin = jnp.zeros((TOK, 1), jnp.int32)
    opening = len_ref[0, 0] * 0
    for n in range(DOCS):
        begin = jnp.where(q_pos >= opening, opening, begin)
        opening = opening + len_ref[0, n]
    k_pos = first - TOK + lax.broadcasted_iota(jnp.int32, (TOK, 2 * TOK), 1)
    bias[...] = jnp.where((k_pos >= begin) & (k_pos <= q_pos), 0.0, -1e30)
    gk_t[...] = jnp.zeros_like(gk_t)
    gv_t[...] = jnp.zeros_like(gv_t)

    pl.semaphore_wait(barrier, len(peers))

    prev = pl.ds(0, TOK)
    low, high = pl.ds(0, 64), pl.ds(64, 64)

    def halo(n):
        cols = pl.ds(n // 2 * DH, DH)
        source = (k_hbm, v_hbm)[n % 2]
        return HALO + n, source.at[:, cols], kv.at[n % 2, prev, cols], after

    for n in range(8):
        send(*halo(n))
    send(WX, w_hbm.at[c, low], wf.at[d, c, low], to_x(1))
    send(WX + 2, w_hbm.at[c, high], wf.at[d, c, high], to_x(3))
    send(WX + 1, w_hbm.at[c, high], wf.at[d, c, high], to_x(1))
    send(WX + 3, w_hbm.at[c, low], wf.at[d, c, low], to_x(3))
    send(WZ, w_hbm.at[c, low], wf.at[d, c, low], near)
    send(WZ + 1, w_hbm.at[c, high], wf.at[d, c, high], far)
    send(COT, cot_hbm.at[:, pl.ds(pl.multiple_of((1 - c) * 1024, 1024), 1024)], cotm, mate)

    def shard_x(i, plane):
        return plane * 4 + turn(x, (0, 3, 1, 2)[i])

    def part_x(n, i, part, relay=None):
        piece = wf.at[shard_x(i, zl), c, part]
        rc(WX + n, piece, piece, mate).wait_recv()
        if relay is not None:
            send(WX + relay[0], piece, piece, to_x(relay[1]))
        if part is low:
            send(WZ + 2 * i, piece, piece, near)
        else:
            send(WZ + 2 * i + 1, piece, piece, far)

    def to_mate(j, e):
        send(WC + j, wf.at[e, c], wf.at[e, c], mate)

    def forward_x(step):
        if step == 0:
            part_x(0, 1, low, (4, 1))
            part_x(2, 2, high, (5, 3))
        if step == 1:
            part_x(1, 1, high)
            part_x(3, 2, low)
            to_mate(0, shard_x(1, zl))
            to_mate(1, shard_x(2, zl))
        if step == 2:
            part_x(4, 3, low)
            part_x(5, 3, high)
            to_mate(2, shard_x(3, zl))

    def forward_z(i):
        e = shard_x(i, 1 - zl)
        rc(WZ + 2 * i, wf.at[e, c, low], wf.at[e, c, low], mate).wait_recv()
        rc(WZ + 2 * i + 1, wf.at[e, c, high], wf.at[e, c, high], mate).wait_recv()
        to_mate(3 + i, e)

    def from_mate(j, e):
        rc(WC + j, wf.at[e, 1 - c], wf.at[e, 1 - c], mate).wait_recv()

    for load in loads[:3]:
        load.wait()

    class Ring:
        def __init__(self, base, v, to, piece, slot):
            self.base, self.v, self.piece, self.slot = base, v, piece, slot
            self.up, self.down = to(1), to(3)

        def start(self):
            v, piece, slot = self.v, self.piece, self.slot
            send(self.base, piece(turn(v, 2), 0), slot(0), self.up)
            send(self.base + 1, piece(turn(v, 2), 1), slot(1), self.down)
            send(self.base + 2, piece(turn(v, 1), 1), slot(2), self.up)
            send(self.base + 3, piece(turn(v, 3), 0), slot(3), self.down)

        def relay(self):
            for part, n, to in ((0, 1, self.up), (1, 3, self.down)):
                mid, got = self.piece(turn(self.v, n), part), self.slot(part)
                rc(self.base + part, got, got, mate).wait_recv()
                mid[...] = (mid[...].astype(F32) + got[...].astype(F32)).astype(BF16)
                send(self.base + 4 + part, mid, self.slot(4 + part), to)

        def wait(self):
            for n in range(2, 6):
                rc(self.base + n, self.slot(n), self.slot(n), mate).wait_recv()

    def ring_of_y(k):
        return Ring(
            Y1 + 6 * k, y, to_y, lambda to, part: g_y.at[to, 2 * k + part], lambda n: r_y1.at[n, k]
        )

    ring_y = [ring_of_y(k) for k in range(HK)]
    ring_x = Ring(X1, x, to_x, lambda to, part: g_x.at[to, part], lambda n: r_x1.at[n])
    ring_z = Ring(Z1, z, to_z, lambda to, part: g_z.at[to, part], lambda n: r_z1.at[n])

    def head(h):
        return pl.ds(pl.multiple_of(h * DH, DH), DH)

    def fwd(k):
        for n in (2 * k, 2 * k + 1):
            rc(*halo(n)).wait_recv()
        keys, values = kv[0, :, head(k)], kv[1, :, head(k)]

        wide = jnp.concatenate([values, jnp.ones_like(values)], axis=1)

        def one(g, _):
            h = k * 4 + g
            scores = dg(q_v[:, head(h)], keys, 1, 1) * (SCALE * LOG2E) + bias[...]
            e = jnp.exp2(scores - jnp.max(scores, axis=-1, keepdims=True)).astype(BF16)
            prob[h] = e
            out = dg(e, wide, 1, 0)
            inv = 1.0 / out[:, DH:]
            inverse[:, head(h)] = inv
            att[:, head(h)] = (out[:, :DH] * inv).astype(BF16)
            return 0

        lax.fori_loop(0, 4, one, 0, unroll=True)
        cols = pl.ds(k * 512, 512)
        send(ATT + k, att.at[:, cols], attm.at[:, cols], mate)

    def grad_w(k):
        cols = pl.ds(k * 512, 512)
        rc(ATT + k, att.at[:, cols], attm.at[:, cols], mate).wait_recv()
        if k == 0:
            loads[3].wait()
            rc(COT, cotm, cotm, mate).wait_recv()
        for e in (2 * k, 2 * k + 1):
            own = att[:, e * 256 : (e + 1) * 256]
            other = attm[:, e * 256 : (e + 1) * 256]
            for n in range(4):
                mine = cot_v[:, pl.ds(pl.multiple_of(c * 1024 + n * 256, 256), 256)]
                part = dg(own, mine, 0, 0) + dg(other, cotm[:, n * 256 : (n + 1) * 256], 0, 0)
                part = part.astype(BF16)
                for sub in range(8):
                    rows = part[sub * 32 : (sub + 1) * 32]
                    if n < 2:
                        g_y[sub % 4, e, sub // 4, :, n * 256 : (n + 1) * 256] = rows
                    elif n == 2:
                        g_x[e % 4, e // 4, sub, :, 0:256] = rows
                    else:
                        g_x[e % 4, e // 4, sub, :, 256:384] = rows[:, 0:128]
                        g_z[sub // 4 * 2 + e // 4, e % 4 // 2, e % 2, sub % 4] = rows[:, 128:256]
    fwd(0)
    fwd(1)
    grad_w(0)
    ring_y[0].start()
    forward_x(0)
    fwd(2)
    grad_w(1)
    ring_y[1].start()
    ring_y[0].relay()
    fwd(3)
    grad_w(2)
    ring_y[2].start()
    ring_y[1].relay()
    forward_x(1)
    grad_w(3)
    ring_y[3].start()
    ring_x.start()
    ring_z.start()
    ring_y[2].relay()
    forward_z(0)
    loads[4].wait()

    def bwd(e):
        k = lax.div(e, 2)
        weight = wf[e].reshape(256, DM)
        grad = dg(cot_v[...], weight, 1, 1).astype(BF16)
        keys, values = kv[0, :, head(k)], kv[1, :, head(k)]
        for g in range(2):
            h = 2 * e + g
            grad_h = grad[:, g * DH : (g + 1) * DH]
            delta = jnp.sum(
                grad_h.astype(F32) * att[:, head(h)].astype(F32), axis=-1, keepdims=True
            )
            p = prob[h]
            inv = inverse[:, head(h)]
            grad_n = (grad_h.astype(F32) * inv).astype(BF16)
            inv = jnp.concatenate([inv] * 4, axis=1)
            grad_s = (p.astype(F32) * ((dg(grad_h, values, 1, 1) - delta) * inv)).astype(BF16)
            gq_v[:, head(h)] = (dg(grad_s, keys, 1, 0) * SCALE).astype(BF16)
            gk_t[head(k), :] += dg(q_v[:, head(h)], grad_s, 0, 0)
            gv_t[head(k), :] += dg(grad_n, p, 0, 0)

    def bwd_x(i):
        e = shard_x(i, zl)
        from_mate(i - 1, e)
        bwd(e)

    def bwd_z(i):
        e = shard_x(i, 1 - zl)
        from_mate(3 + i, e)
        bwd(e)

    def arrived(base, dst, source):
        for n in range(3):
            rc(base + n, source, dst.at[n], mate).wait_recv()

    def total(own, got, *where):
        out = own.astype(F32)
        for n in range(3):
            out = out + got[(n, *where)].astype(F32)
        return out

    def settled(own, got, part, *where):
        one, two = ((3, 4), (2, 5))[part]
        return own.astype(F32) + got[(one, *where)].astype(F32) + got[(two, *where)].astype(F32)

    def project(n, _):
        cols = pl.ds(n * 256, 256)
        weight = wf[:, :, :, cols].reshape(2048, 256)
        pro_v[:, cols] = dg(att[...], weight, 1, 0).astype(BF16)
        return 0

    def sum_z():
        ring_z.wait()
        for x_ in range(4):
            for y_ in range(4):
                where = (x_ % 2, y_)
                value = settled(g_z[(z, x_ // 2, *where)], r_z1, x_ // 2, *where)
                s_z[x_, y_] = value.astype(BF16)
        for n in (1, 3, 2):
            send(Z2 + n - 1, s_z.at[turn(x, n)], r_z2.at[n - 1], to_x(n))

    def sum_y():
        for ring in ring_y:
            ring.wait()
        for e in range(8):
            for zh_ in range(2):
                value = settled(g_y[y, e, zh_], r_y1, e % 2, e // 2, zh_)
                s_y[zh_ * 2 + e // 4, e % 4] = value.astype(BF16)
        for n in (1, 3, 2):
            send(Y2 + n - 1, s_y.at[turn(z, n)], r_y2.at[n - 1], to_z(n))

    def sum_x():
        ring_x.wait()
        for zl_ in range(2):
            for sub in range(8):
                value = settled(g_x[x, zl_, sub], r_x1, zl_, sub)
                s_x[sub % 4, sub // 4 * 2 + zl_] = value.astype(BF16)
        for n in (1, 3, 2):
            send(X2 + n - 1, s_x.at[turn(y, n)], r_x2.at[n - 1], to_y(n))

    def give_back(part):
        heads = pl.ds(pl.multiple_of((zl if part == 0 else 1 - zl) * 256, 256), 256)
        back_s[0, :, heads] = (gk_t[heads, 0:TOK].T * SCALE).astype(BF16)
        back_s[1, :, heads] = gv_t[heads, 0:TOK].T.astype(BF16)
        for n in range(2):
            send(BACK + 2 * part + n, back_s.at[n, :, heads], back_r.at[n, :, heads], before)

    bwd(d)
    forward_x(2)
    bwd_x(1)
    bwd_x(2)
    ring_y[3].relay()
    forward_z(1)
    bwd_z(0)
    forward_z(2)
    bwd_x(3)
    give_back(0)
    ring_x.relay()
    ring_z.relay()
    bwd_z(1)
    sum_y()
    bwd_z(2)
    forward_z(3)
    sum_z()
    sum_x()
    bwd_z(3)
    give_back(1)

    for n in range(6):
        project(n, 0)
    arrived(Y2, r_y2, s_y.at[0])
    for x_ in range(4):
        s_y2[x_] = total(s_y[z, x_], r_y2, x_).astype(BF16)
    for n in (1, 3, 2):
        send(Y3 + n - 1, s_y2.at[turn(x, n)], r_y3.at[n - 1], to_x(n))
    arrived(Z2, r_z2, s_z.at[0])
    for y_ in range(4):
        s_z2[y_] = total(s_z[x, y_], r_z2, y_).astype(BF16)
    for n in (1, 3, 2):
        send(Z3 + n - 1, s_z2.at[turn(y, n)], r_z3.at[n - 1], to_y(n))
    arrived(X2, r_x2, s_x.at[0])
    for z_ in range(4):
        s_x2[z_] = total(s_x[y, z_], r_x2, z_).astype(BF16)
    for n in (1, 3, 2):
        send(X3 + n - 1, s_x2.at[turn(z, n)], r_x3.at[n - 1], to_z(n))
    for n in range(6, 8):
        project(n, 0)
    outs = [
        pltpu.make_async_copy(pro_v, pro_hbm, osem.at[0]),
        pltpu.make_async_copy(gq_v, gq_hbm, osem.at[1]),
    ]
    for out in outs:
        out.start()


    factor = 1.0 / math.sqrt(TOTAL)
    piece_of = zh * 4 + y

    def gather(chunk):
        piece = agb.at[chunk, c, piece_of]
        for n in range(7):
            send(AG + 7 * chunk + n, piece, piece, to_y(n + 1) if n < 3 else to_o(n - 3))

    def origin(n):
        return zh * 4 + turn(y, 3 - n) if n < 3 else (1 - zh) * 4 + turn(y, 7 - n)

    def gathered(chunk, part):
        for n in (range(3), range(3, 7))[part]:
            piece = agb.at[chunk, c, origin(n)]
            rc(AG + 7 * chunk + n, piece, piece, mate).wait_recv()
        which = zh if part == 0 else 1 - zh
        half = agb.at[chunk, c, pl.ds(which * 4, 4)]
        send(AGC + 2 * chunk + part, half, half, mate)

    def finished(chunk):
        for part, which in enumerate((zh, 1 - zh)):
            half = agb.at[chunk, 1 - c, pl.ds(which * 4, 4)]
            rc(AGC + 2 * chunk + part, half, half, mate).wait_recv()
        outs.append(pltpu.make_async_copy(agb.at[chunk], gw_hbm.at[chunk], osem.at[4 + chunk]))
        outs[-1].start()

    arrived(Y3, r_y3, s_y2.at[0])
    agb[0, c, piece_of] = (total(s_y2[x], r_y3) * factor).astype(BF16)
    gather(0)
    arrived(Z3, r_z3, s_z2.at[0])
    agb[1, c, piece_of, :, 384:512] = (total(s_z2[y], r_z3) * factor).astype(BF16)
    arrived(X3, r_x3, s_x2.at[0])
    agb[1, c, piece_of, :, 0:384] = (total(s_x2[z], r_x3) * factor).astype(BF16)
    gather(1)

    for part in range(2):
        heads = pl.ds(pl.multiple_of((zl if part == 0 else 1 - zl) * 256, 256), 256)
        for n in range(2):
            got = back_r.at[n, :, heads]
            rc(BACK + 2 * part + n, got, got, before).wait_recv()
    gkv_v[0] = (gk_t[:, TOK : 2 * TOK].T * SCALE + back_r[0].astype(F32)).astype(BF16)
    gkv_v[1] = (gv_t[:, TOK : 2 * TOK].T + back_r[1].astype(F32)).astype(BF16)
    for n, out in enumerate((gk_hbm, gv_hbm)):
        outs.append(pltpu.make_async_copy(gkv_v.at[n], out, osem.at[2 + n]))
        outs[-1].start()

    gathered(0, 0)
    gathered(1, 0)
    gathered(0, 1)
    finished(0)
    gathered(1, 1)
    finished(1)
    for copy in sent:
        copy.wait_send()
    for out in outs:
        out.wait()


def finish(
    pro, gq, gk, gv, gw, pro_o, gq_o, gk_o, gv_o, gw_o,
    pro_v, gq_v, gk_v, gv_v, gw_v, wide, in_sem, out_sem,
):
    pieces = [(gw.at[a, b], gw_v.at[a, b], (a, b)) for a in range(2) for b in range(2)]
    for source, held, out in ((pro, pro_v, pro_o), (gq, gq_v, gq_o)):
        for n in range(2):
            rows = pl.ds(n * 128, 128)
            pieces.append((source.at[rows], held.at[rows], out.at[rows]))
    pieces += [(gk, gk_v, gk_o), (gv, gv_v, gv_o)]
    got = [
        pltpu.make_async_copy(source, held, in_sem.at[n])
        for n, (source, held, _) in enumerate(pieces)
    ]
    for copy in got:
        copy.start()
    put = []
    for n, (_, held, out) in enumerate(pieces):
        got[n].wait()
        if n < 4:
            a, b = out
            cols = pl.ds(b * 1024 + a * 512, 512)
            wide[:, cols] = gw_v[a, b].reshape(TOK, 512).astype(F32)
            held, out = wide.at[:, cols], gw_o.at[:, cols]
        put.append(pltpu.make_async_copy(held, out, out_sem.at[n]))
        put[n].start()
    for copy in put:
        copy.wait()


def body(queries, key_heads, value_heads, doc_lengths, out_weight, cotangent):
    anywhere = pl.BlockSpec(memory_space=pl.ANY)
    shapes = [
        ((TOK, 2048), BF16),
        ((TOK, 2048), BF16),
        ((2, 512, 512), BF16),
        ((8, 2, 128, 2048), BF16),
        ((TOK, 1024), BF16),
        ((TOK, 2048), BF16),
        ((TOK, 2048), BF16),
        ((HQ, TOK, 512), BF16),
        ((TOK, 512), F32),
        ((TOK, 2048), F32),
        ((4, 8, 2, 32, 512), BF16),
        ((6, 4, 2, 32, 512), BF16),
        ((4, 4, 32, 512), BF16),
        ((3, 4, 32, 512), BF16),
        ((4, 32, 512), BF16),
        ((3, 32, 512), BF16),
        ((4, 2, 8, 32, 384), BF16),
        ((6, 8, 32, 384), BF16),
        ((4, 4, 32, 384), BF16),
        ((3, 4, 32, 384), BF16),
        ((4, 32, 384), BF16),
        ((3, 32, 384), BF16),
        ((4, 2, 2, 4, 32, 128), BF16),
        ((6, 2, 4, 32, 128), BF16),
        ((4, 4, 32, 128), BF16),
        ((3, 4, 32, 128), BF16),
        ((4, 32, 128), BF16),
        ((3, 32, 128), BF16),
        ((2, 2, 8, 32, 512), BF16),
        ((512, 512), F32),
        ((512, 512), F32),
        ((2, TOK, 512), BF16),
        ((2, TOK, 512), BF16),
        ((TOK, 2048), BF16),
        ((TOK, 2048), BF16),
        ((2, TOK, 512), BF16),
    ]
    scratch = [pltpu.VMEM(shape, dtype) for shape, dtype in shapes]
    scratch += [pltpu.SemaphoreType.DMA((n,)) for n in (COPIES, COPIES, 5, 6)]
    results = [
        jax.ShapeDtypeStruct((TOK, 2048), BF16),
        jax.ShapeDtypeStruct((TOK, 2048), BF16),
        jax.ShapeDtypeStruct((TOK, 512), BF16),
        jax.ShapeDtypeStruct((TOK, 512), BF16),
    ]
    outs = pl.pallas_call(
        kernel,
        out_shape=[*results, jax.ShapeDtypeStruct((2, 2, 8, 32, 512), BF16)],
        in_specs=[pl.BlockSpec(memory_space=pltpu.SMEM)] + [anywhere] * 5,
        out_specs=[anywhere] * 5,
        scratch_shapes=scratch,
        compiler_params=pltpu.CompilerParams(
            collective_id=0, has_side_effects=True, vmem_limit_bytes=56 << 20
        ),
        cost_estimate=pl.CostEstimate(
            flops=10_000_000_000, bytes_accessed=12_000_000, transcendentals=2_000_000
        ),
    )(
        doc_lengths,
        queries[0],
        key_heads[0],
        value_heads[0],
        out_weight.reshape(2, 128, DM),
        cotangent[0],
    )
    outs = pl.pallas_call(
        finish,
        out_shape=[*results, jax.ShapeDtypeStruct((TOK, 2048), F32)],
        in_specs=[anywhere] * 5,
        out_specs=[anywhere] * 5,
        scratch_shapes=[
            *(pltpu.VMEM(result.shape, BF16) for result in results),
            pltpu.VMEM((2, 2, 8, 32, 512), BF16),
            pltpu.VMEM((TOK, 2048), F32),
            pltpu.SemaphoreType.DMA((10,)),
            pltpu.SemaphoreType.DMA((10,)),
        ],
    )(*outs)
    return (*(out[None] for out in outs[:4]), outs[4])


def solution(mesh):
    tokens = P("dp", "seq", None)
    rows = P("dp", None)
    return jax.shard_map(
        body,
        mesh=mesh,
        in_specs=(tokens, tokens, tokens, rows, rows, tokens),
        out_specs=(tokens, tokens, tokens, tokens, rows),
        check_vma=False,
    )
```
